512 devices in a mesh: seq: 128 (over x, z, y_lo), chan: 4 (over y_hi, core).
Axes of the slice: x: 4, y: 8 (y_hi: 2, y_lo: 4; y = y_hi * 4 + y_lo), z: 8, core: 2. Of those that a mesh axis runs over, the one named last changes fastest.
Arguments:
- inputs: bfloat16 [512, 512, 1024], P('seq', None, 'chan'), may hold values from -33 to 33
- norm_gain: float32 [1024], P('chan'), may hold values from 0.1 to 1.9
- inner_factor: bfloat16 [512, 512], replicated, may hold values from -0.25 to 0.25
- outer_factor: bfloat16 [512, 512], replicated, may hold values from -0.25 to 0.25
- twiddle: float32 [512, 512], P('seq'), may hold values from 0.5 to 2
- channel_weight: bfloat16 [4, 256, 256], P('chan'), may hold values from -0.375 to 0.375
- cotangent: bfloat16 [512, 512, 1024], P('seq', None, 'chan'), may hold values from -6 to 6
Outputs:
- input_grad: bfloat16 [512, 512, 1024], P('seq', None, 'chan')
- weight_grad: float32 [4, 256, 256], P('chan')
The draws below stay inside these ranges and needn't reach their ends.
All inputs are finite; a program needn't handle non-finite values.
Results may differ from the reference program's by a relative error of at most 0.0071.
Values may be sent and summed in bfloat16 or wider, within the bound.
No kernel may reach another device: no remote copies, remote signals or barrier semaphores. Data moves between devices by JAX's collectives and lax.ppermute only.
A program may use at most 64 MiB of HBM per device.

```python
from functools import partial
import jax
import jax.numpy as jnp
from jax import lax

N1 = 512
N2 = 512
D = 1024
BLOCKS = 4
BW = 256


def draw_inputs(key, part):
    key_base, key_rows, key_cols = jax.random.split(key, 3)
    base = jnp.clip(jax.random.normal(key_base, (N1, N2, D), jnp.float32), -6.0, 6.0)
    rows = 10.0 ** jax.random.uniform(key_rows, (N1, N2, 1), jnp.float32, -1.0, 0.0)
    ramp = 3.0 ** (jnp.arange(D, dtype=jnp.float32) / D - 0.5)
    cols = 10.0 ** jax.random.uniform(key_cols, (D,), jnp.float32, -0.5, 0.5) * ramp
    return (base * rows * cols).astype(jnp.bfloat16)


def block_scale(rng, dims, pieces, smallest, high):
    gain = 1.0
    for dim, shards_of in pieces:
        draws = jax.random.uniform(jax.random.fold_in(jax.random.fold_in(rng, 6), dim), (shards_of,), jnp.float32, smallest / len(pieces), high / len(pieces))
        gain = gain * jnp.repeat(jnp.exp(draws), dims[dim] // shards_of).reshape((-1,) + (1,) * (len(dims) - 1 - dim))
    return gain


def noise(stream_key, dims, width, limit, cuts=(), kind=jnp.bfloat16):
    factor_of = block_scale(stream_key, dims, cuts, -0.22, 0.18) if cuts else 1.0
    drawn = jax.random.normal(stream_key, dims, jnp.float32) * width * factor_of
    return jnp.minimum(jnp.maximum(drawn, -limit), limit).astype(kind)


def setup_inputs(seed: int = 0) -> dict:
    keys = jax.random.split(jax.random.key(seed), 8)
    inputs = draw_inputs(jax.random.fold_in(keys[7], 71), 0)
    norm_gain = jnp.clip(1.0 + 0.18 * jax.random.normal(keys[1], (D,), jnp.float32), 0.1, 1.9)
    inner_factor = noise(keys[2], (N2, N2), N2 ** -0.5, 0.25)
    outer_factor = noise(keys[3], (N1, N1), N1 ** -0.5, 0.25)
    twiddle = jnp.clip(0.5 + 1.5 * jax.random.uniform(keys[4], (N1, N2), jnp.float32) ** block_scale(keys[4], (N1, N2), ((0, 128),), -0.2, 0.2), 0.5, 2.0)
    channel_weight = noise(keys[5], (BLOCKS, BW, BW), BW ** -0.5, 0.375, ((0, 4),))
    cotangent = noise(keys[6], (N1, N2, D), 1.0, 6.0, ((0, 128), (2, 4)))
    return {"inputs": inputs, "norm_gain": norm_gain, "inner_factor": inner_factor, "outer_factor": outer_factor, "twiddle": twiddle, "channel_weight": channel_weight, "cotangent": cotangent}


GELU_C = 0.7978845608028654
GELU_A = 0.044715

def gelu_value(v):
    return 0.5 * v * (1.0 + jnp.tanh(GELU_C * (v + GELU_A * v * v * v)))

def gelu_slope(v):
    t = jnp.tanh(GELU_C * (v + GELU_A * v * v * v))
    return 0.5 * (1.0 + t) + 0.5 * v * (1.0 - t * t) * GELU_C * (1.0 + 3.0 * GELU_A * v * v)

def block_grads(inv_rms, twiddle, inner_factor, outer_factor, items):
    x_blk, cot_blk, gain_blk, weight_blk = items
    x_wide = x_blk.astype(jnp.float32)
    normed = (x_wide * inv_rms[..., None] * gain_blk).astype(jnp.bfloat16)
    inner_wide = inner_factor.astype(jnp.float32)
    outer_wide = outer_factor.astype(jnp.float32)
    rotated = (twiddle[..., None] * jnp.einsum('ji,rid->rjd', inner_wide, normed.astype(jnp.float32))).astype(jnp.bfloat16)
    mixed = jnp.einsum('ji,icd->jcd', outer_wide, rotated.astype(jnp.float32)).astype(jnp.bfloat16)
    mixed_wide = mixed.astype(jnp.float32)
    hidden = gelu_value(mixed_wide).astype(jnp.bfloat16)
    cot_flat = cot_blk.reshape(-1, BW)
    hidden_grad = jnp.dot(cot_flat, weight_blk.T, preferred_element_type=jnp.float32).reshape(N1, N2, BW)
    weight_part = jnp.dot(hidden.reshape(-1, BW).T, cot_flat, preferred_element_type=jnp.float32)
    mixed_grad = (hidden_grad * gelu_slope(mixed_wide)).astype(jnp.bfloat16)
    rotated_grad = jnp.einsum('ji,jcd->icd', outer_wide, mixed_grad.astype(jnp.float32)).astype(jnp.bfloat16)
    scaled_grad = (twiddle[..., None] * rotated_grad.astype(jnp.float32)).astype(jnp.bfloat16)
    normed_grad = jnp.einsum('ji,rjd->rid', inner_wide, scaled_grad.astype(jnp.float32))
    proj_part = lax.optimization_barrier(jnp.sum(normed_grad * gain_blk * x_wide, axis=-1))
    return (normed_grad, proj_part, weight_part)

def reference(inputs, norm_gain, inner_factor, outer_factor, twiddle, channel_weight, cotangent):
    sq_mean = lax.optimization_barrier(jnp.sum(jnp.square(inputs.astype(jnp.float32)), axis=-1)) / D
    inv_rms = lax.rsqrt(sq_mean + 1e-05)
    x_blocks = jnp.moveaxis(inputs.reshape(N1, N2, BLOCKS, BW), 2, 0)
    cot_blocks = jnp.moveaxis(cotangent.reshape(N1, N2, BLOCKS, BW), 2, 0)
    gain_blocks = norm_gain.reshape(BLOCKS, BW)
    worker = partial(block_grads, inv_rms, twiddle, inner_factor, outer_factor)
    normed_grad, proj_parts, weight_grad = lax.map(worker, (x_blocks, cot_blocks, gain_blocks, channel_weight))
    projection = lax.optimization_barrier(jnp.sum(proj_parts, axis=0))

    def finish(items):
        x_blk, cot_blk, gain_blk, grad_blk = items
        x_wide = x_blk.astype(jnp.float32)
        result = cot_blk.astype(jnp.float32) + inv_rms[..., None] * gain_blk * grad_blk - x_wide * (inv_rms ** 3)[..., None] * projection[..., None] / D
        return result.astype(jnp.bfloat16)
    grad_blocks = lax.map(finish, (x_blocks, cot_blocks, gain_blocks, normed_grad))
    input_grad = jnp.moveaxis(grad_blocks, 0, 2).reshape(N1, N2, D)
    return (input_grad, weight_grad)
```

```python
import jax
import jax.numpy as jnp
from jax import lax
from jax.sharding import PartitionSpec as P

D = 1024


GELU_C = 0.7978845608028654
GELU_A = 0.044715


def gelu_value(v):
    return 0.5 * v * (1.0 + jnp.tanh(GELU_C * (v + GELU_A * v * v * v)))


def gelu_slope(v):
    t = jnp.tanh(GELU_C * (v + GELU_A * v * v * v))
    return 0.5 * (1.0 + t) + 0.5 * v * (1.0 - t * t) * GELU_C * (1.0 + 3.0 * GELU_A * v * v)


def exchange(v):
    return lax.all_to_all(v, "seq", split_axis=0, concat_axis=0, tiled=True)


def to_columns(v, seq):
    r, n2, d = v.shape
    v = v.reshape(r, n2 // seq, seq, d).transpose(2, 0, 1, 3)
    return exchange(v.reshape(seq, r, -1)).reshape(seq * r, n2 // seq, d)


def on_device(seq, inputs, norm_gain, inner_factor, outer_factor, twiddle, channel_weight, cotangent):
    rows, n2, width = inputs.shape
    nh = n2 // seq
    cot = to_columns(cotangent, seq)
    x_wide = inputs.astype(jnp.float32)
    sq_sum = lax.psum(jnp.sum(x_wide * x_wide, axis=-1), "chan")
    inv_rms = lax.rsqrt(sq_sum / D + 1e-05)
    normed = (x_wide * inv_rms[..., None] * norm_gain).astype(jnp.bfloat16)
    inner_out = jnp.einsum("ji,rid->rjd", inner_factor, normed, preferred_element_type=jnp.float32)
    rotated = (twiddle[..., None] * inner_out).astype(jnp.bfloat16)
    mixed = jnp.einsum(
        "ji,ihd->jhd", outer_factor, to_columns(rotated, seq), preferred_element_type=jnp.float32
    ).astype(jnp.bfloat16)
    mixed_wide = mixed.astype(jnp.float32)
    hidden = gelu_value(mixed_wide).astype(jnp.bfloat16)
    weight = channel_weight[0]
    hidden_grad = jnp.einsum("jhm,km->jhk", cot, weight, preferred_element_type=jnp.float32)
    weight_part = jnp.einsum("jhk,jhm->km", hidden, cot, preferred_element_type=jnp.float32)
    mixed_grad = (hidden_grad * gelu_slope(mixed_wide)).astype(jnp.bfloat16)
    rotated_grad = jnp.einsum(
        "ji,jhd->ihd", outer_factor, mixed_grad, preferred_element_type=jnp.float32
    ).astype(jnp.bfloat16)
    back = exchange(rotated_grad.reshape(seq, rows, nh * width))
    back = back.reshape(seq, rows, nh, width).transpose(1, 2, 0, 3).reshape(rows, n2, width)
    scaled = (twiddle[..., None] * back.astype(jnp.float32)).astype(jnp.bfloat16)
    normed_grad = jnp.einsum("ji,rjd->rid", inner_factor, scaled, preferred_element_type=jnp.float32)
    projection = lax.psum(jnp.sum(normed_grad * norm_gain * x_wide, axis=-1), "chan")
    input_grad = (
        cotangent.astype(jnp.float32)
        + inv_rms[..., None] * norm_gain * normed_grad
        - x_wide * (inv_rms**3)[..., None] * projection[..., None] / D
    )
    pieces = exchange(weight_part.reshape(seq, width // seq, width))
    share = jnp.sum(pieces, axis=0)
    whole = exchange(jnp.broadcast_to(share, (seq,) + share.shape))
    return (input_grad.astype(jnp.bfloat16), whole.reshape(1, width, width))


def solution(mesh):
    in_specs = (
        P("seq", None, "chan"),
        P("chan"),
        P(),
        P(),
        P("seq", None),
        P("chan", None, None),
        P("seq", None, "chan"),
    )
    out_specs = (P("seq", None, "chan"), P("chan", None, None))

    def run(*args):
        return on_device(mesh.shape["seq"], *args)

    return jax.shard_map(run, mesh=mesh, in_specs=in_specs, out_specs=out_specs, check_vma=False)
```

```python
import functools

import jax
import jax.numpy as jnp
from jax import lax
from jax.experimental import pallas as pl
from jax.experimental.pallas import tpu as pltpu
from jax.sharding import PartitionSpec as P

D = 1024
GELU_C = 0.7978845608028654
GELU_A = 0.044715
F32 = jnp.float32
BF16 = jnp.bfloat16
LANES = 128


def dot(a, b, ca, cb):
    return lax.dot_general(a, b, (((ca,), (cb,)), ((), ())), preferred_element_type=F32)


def lane_sums(v):
    ones = jnp.ones((8, v.shape[1]), BF16)
    hi = v.astype(BF16)
    rest = v - hi.astype(F32)
    return dot(ones, hi, 1, 1) + dot(ones, rest.astype(BF16), 1, 1)


def column_form(v):
    r, n = v.shape
    return jnp.concatenate([v] * (8 // r), axis=0).T


class Sizes:
    def __init__(self, seq, rows, n2, width):
        self.seq, self.rows, self.n2, self.width = seq, rows, n2, width
        self.cols = n2 // seq
        self.parts = width // LANES
        self.block = self.cols * self.parts * rows
        self.extra = 2 * (width // seq) * self.parts

    def pieces(self):
        for jh in range(self.cols):
            for part in range(self.parts):
                yield jh, part, (jh * self.parts + part) * self.rows


def square_kernel(s, x_ref, sum_ref):
    for r in range(s.rows):
        x = x_ref[r].astype(F32)
        sum_ref[r : r + 1, :] = lane_sums(x * x)[0:1]


def inner_kernel(s, x_ref, cot_ref, sum_ref, gain_ref, inner_ref, tw_ref, send_ref, inv_ref, wide_ref):
    inv = lax.rsqrt(sum_ref[...] / D + 1e-05)
    inv_ref[...] = inv
    inv_cols = column_form(inv)
    tw_cols = column_form(tw_ref[...])
    for r in range(s.rows):
        normed = (x_ref[r].astype(F32) * inv_cols[:, r : r + 1] * gain_ref[...]).astype(BF16)
        y = dot(inner_ref[...], normed, 1, 0) * tw_cols[:, r : r + 1]
        cot = cot_ref[r].astype(F32)
        for jh, part, q in s.pieces():
            here = slice(jh * s.seq, (jh + 1) * s.seq), slice(part * LANES, (part + 1) * LANES)
            wide_ref[pl.ds(q + r, s.seq, 2 * s.block), :] = y[here]
            wide_ref[pl.ds(s.block + q + r, s.seq, 2 * s.block), :] = cot[here]
    send_ref[...] = wide_ref[...].astype(BF16)


def swap_halves(first, second):
    low = lax.broadcasted_iota(jnp.int32, first.shape, 1) < 4
    return (
        jnp.where(low, first, pltpu.roll(second, 4, 1)),
        jnp.where(low, pltpu.roll(first, 4, 1), second),
    )


def unit(n):
    a = lax.broadcasted_iota(jnp.int32, (n, n), 0)
    return jnp.where(a == lax.broadcasted_iota(jnp.int32, (n, n), 1), 1.0, 0.0).astype(BF16)


def middle_kernel(s, got_ref, weight_ref, outer_ref, send_ref, part_ref, out_ref):
    n1 = s.seq * s.rows
    outer_t = dot(unit(n1), outer_ref[...], 1, 1).astype(BF16)
    tiles = s.block // 8
    got = got_ref[...].reshape(s.seq // 2, 2, 2 * tiles, 8, LANES)
    for jh in range(s.cols):
        rot, cot = (
            jnp.concatenate(
                [
                    v.reshape(n1, LANES)
                    for v in swap_halves(got[:, 0, tile].astype(F32), got[:, 1, tile].astype(F32))
                ],
                axis=1,
            ).astype(BF16)
            for tile in (jh, tiles + jh)
        )
        v = dot(outer_ref[...], rot, 1, 0).astype(BF16).astype(F32)
        t = jnp.tanh(GELU_C * (v + GELU_A * v * v * v))
        hidden = (0.5 * v * (1.0 + t)).astype(BF16)
        slope = 0.5 * (1.0 + t) + 0.5 * v * (1.0 - t * t) * GELU_C * (1.0 + 3.0 * GELU_A * v * v)
        grad = (dot(cot, weight_ref[...], 1, 1) * slope).astype(BF16)
        product = dot(hidden, cot, 0, 0)
        for part in range(s.parts):
            here = slice(part * s.width, (part + 1) * s.width)
            term = product[:, part * LANES : (part + 1) * LANES]
            part_ref[here, :] = term if jh == 0 else part_ref[here, :] + term
        back = dot(outer_t, grad, 1, 0)
        even, odd = swap_halves(
            back[:, :LANES].reshape(n1 // 8, 8, LANES), back[:, LANES:].reshape(n1 // 8, 8, LANES)
        )
        out_ref[:, 0, jh] = even
        out_ref[:, 1, jh] = odd
    step = s.width // s.seq
    flat = out_ref.reshape(s.seq * (s.block + s.extra), LANES)
    for i in range(step):
        for part in range(s.parts):
            at = s.block + i * s.parts + part
            v = part_ref[pl.ds(part * s.width + i, s.seq, step), :]
            hi = v.astype(BF16).astype(F32)
            flat[pl.ds(at, s.seq, s.block + s.extra), :] = hi
            flat[pl.ds(at + s.extra // 2, s.seq, s.block + s.extra), :] = v - hi
    send_ref[...] = flat[...].astype(BF16)


def back_kernel(s, got_ref, x_ref, cot_ref, inv_ref, gain_ref, tw_ref, inner_ref, sum_ref, proj_ref, wide_ref, col_ref):
    inner_t = dot(unit(s.n2), inner_ref[...], 1, 1).astype(BF16)
    wide_ref[...] = got_ref[...].astype(F32)
    full = s.block + s.extra
    inv_cols = column_form(inv_ref[...])
    tw_cols = column_form(tw_ref[...])
    for r in range(s.rows):
        for jh, part, q in s.pieces():
            here = slice(jh * s.seq, (jh + 1) * s.seq)
            col_ref[here, part * LANES : (part + 1) * LANES] = (
                wide_ref[pl.ds(q + r, s.seq, full), :] * tw_cols[here, r : r + 1]
            ).astype(BF16)
        grad = dot(inner_t, col_ref[...], 1, 0)
        gained = grad * gain_ref[...]
        proj_ref[r : r + 1, :] = lane_sums(gained * x_ref[r].astype(F32))[0:1]
        sum_ref[r] = cot_ref[r].astype(F32) + inv_cols[:, r : r + 1] * gained


def finish_kernel(s, sum_ref, x_ref, inv_ref, proj_ref, whole_ref, out_ref, weight_ref):
    for part in range(s.parts):
        weight_ref[:, part * LANES : (part + 1) * LANES] = whole_ref[pl.ds(part, s.width, s.parts), :]
    inv = inv_ref[...]
    factor = column_form(inv * inv * inv * proj_ref[...] / D)
    for r in range(s.rows):
        out_ref[r] = (sum_ref[r] - x_ref[r].astype(F32) * factor[:, r : r + 1]).astype(BF16)


def call(kernel, s, name, outs, scratch, flops, moved, *args):
    return pl.pallas_call(
        functools.partial(kernel, s),
        out_shape=[jax.ShapeDtypeStruct(shape, kind) for shape, kind in outs],
        scratch_shapes=[pltpu.VMEM(shape, kind) for shape, kind in scratch],
        compiler_params=pltpu.CompilerParams(vmem_limit_bytes=60 << 20),
        cost_estimate=pl.CostEstimate(flops=flops, bytes_accessed=moved, transcendentals=0),
        name=name,
    )(*args)


def exchange(v, seq):
    packed = v.reshape(seq, -1, LANES)
    return lax.all_to_all(packed, "seq", split_axis=0, concat_axis=0, tiled=True).reshape(v.shape)


def on_device(seq, inputs, norm_gain, inner_factor, outer_factor, twiddle, channel_weight, cotangent):
    rows, n2, width = inputs.shape
    s = Sizes(seq, rows, n2, width)
    packed_two = (2 * seq * s.block, LANES)
    packed_more = (seq * (s.block + s.extra), LANES)
    mib = rows * n2 * width * 2
    flop = 2 * rows * n2 * n2 * width
    gain = norm_gain.reshape(1, width)
    weight = channel_weight[0]
    (part_sum,) = call(square_kernel, s, "squares", [((rows, n2), F32)], [], flop // 20, mib, inputs)
    sq_sum = lax.psum(part_sum, "chan")
    send, inv = call(
        inner_kernel, s, "inner", [(packed_two, BF16), ((rows, n2), F32)], [(packed_two, F32)], flop, 5 * mib,
        inputs, cotangent, sq_sum, gain, inner_factor, twiddle,
    )
    got = exchange(send, seq)
    (back_send,) = call(
        middle_kernel, s, "middle", [(packed_more, BF16)],
        [((s.parts * width, LANES), F32), ((seq // 2, 2, (s.block + s.extra) // 8, 8, LANES), F32)], 3 * flop, 4 * mib,
        got, weight, outer_factor,
    )
    back_got = exchange(back_send, seq)
    pairs = back_got.reshape(seq, s.block + s.extra, LANES)[:, s.block :].astype(F32)
    pairs = jnp.sum(pairs, axis=0)
    share = pairs[: s.extra // 2] + pairs[s.extra // 2 :]
    whole = lax.all_to_all(
        jnp.broadcast_to(share, (seq,) + share.shape), "seq", split_axis=0, concat_axis=0, tiled=True
    )
    base, part_proj = call(
        back_kernel, s, "back", [(inputs.shape, F32), ((rows, n2), F32)],
        [(packed_more, F32), ((n2, width), BF16)], flop, 6 * mib,
        back_got, inputs, cotangent, inv, gain, twiddle, inner_factor,
    )
    projection = lax.psum(part_proj, "chan")
    input_grad, weight_grad = call(
        finish_kernel, s, "finish", [(inputs.shape, BF16), ((width, width), F32)], [], flop // 100, 4 * mib,
        base, inputs, inv, projection, whole.reshape(-1, LANES),
    )
    return (input_grad, weight_grad.reshape(1, width, width))


def solution(mesh):
    in_specs = (
        P("seq", None, "chan"),
        P("chan"),
        P(),
        P(),
        P("seq", None),
        P("chan", None, None),
        P("seq", None, "chan"),
    )
    out_specs = (P("seq", None, "chan"), P("chan", None, None))

    def run(*args):
        return on_device(mesh.shape["seq"], *args)

    return jax.shard_map(run, mesh=mesh, in_specs=in_specs, out_specs=out_specs, check_vma=False)
```

```python
import functools

import jax
import jax.numpy as jnp
from jax import lax
from jax.experimental import pallas as pl
from jax.experimental.pallas import tpu as pltpu
from jax.sharding import PartitionSpec as P

D = 1024
GELU_C = 0.7978845608028654
GELU_A = 0.044715
F32 = jnp.float32
BF16 = jnp.bfloat16
LANES = 128
CHUNKS = 4


def dot(a, b, ca, cb):
    return lax.dot_general(a, b, (((ca,), (cb,)), ((), ())), preferred_element_type=F32)


def lane_sums(v):
    ones = jnp.ones((8, v.shape[1]), BF16)
    hi = v.astype(BF16)
    rest = v - hi.astype(F32)
    return dot(ones, hi, 1, 1) + dot(ones, rest.astype(BF16), 1, 1)


def column_form(v):
    r, n = v.shape
    return jnp.concatenate([v] * (8 // r), axis=0).T


class Sizes:
    def __init__(self, seq, rows, n2, width):
        self.seq, self.rows, self.n2, self.width = seq, rows, n2, width
        self.cols = n2 // seq
        self.parts = width // LANES
        self.block = self.cols * self.parts * rows
        self.extra = 2 * (width // seq) * self.parts

    def pieces(self):
        for jh in range(self.cols):
            for part in range(self.parts):
                yield jh, part, (jh * self.parts + part) * self.rows


class Copies:
    def __init__(self, sems):
        self.sems, self.all = sems, []

    def start(self, source, target):
        copy = pltpu.make_async_copy(source, target, self.sems.at[len(self.all)])
        copy.start()
        self.all.append(copy)
        return copy

    def rows(self, source, target, count):
        return [self.start(source.at[r], target.at[r]) for r in range(count)]


def wait(copies):
    for copy in copies:
        copy.wait()


def square_kernel(s, x_hbm, sum_ref, x_ref, sems):
    loads = Copies(sems).rows(x_hbm, x_ref, s.rows)
    for r in range(s.rows):
        loads[r].wait()
        x = x_ref[r].astype(F32)
        sum_ref[r : r + 1, :] = lane_sums(x * x)[0:1]


def inner_kernel(
    s, x_hbm, cot_hbm, inner_hbm, sum_ref, gain_ref, tw_ref, send_hbm, inv_ref,
    x_ref, cot_ref, inner_ref, wide_ref, wide_cot_ref, buf_ref, buf_cot_ref, sems,
):
    copies = Copies(sems)
    cot_loads = copies.rows(cot_hbm, cot_ref, s.rows)
    inner_load = copies.start(inner_hbm, inner_ref)
    x_loads = copies.rows(x_hbm, x_ref, s.rows)
    inv = lax.rsqrt(sum_ref[...] / D + 1e-05)
    inv_ref[...] = inv
    inv_cols = column_form(inv)
    tw_cols = column_form(tw_ref[...])
    for r in range(s.rows):
        cot_loads[r].wait()
        for jh, part, q in s.pieces():
            wide_cot_ref[pl.ds(q + r, s.seq, s.block), :] = cot_ref[
                r, jh * s.seq : (jh + 1) * s.seq, part * LANES : (part + 1) * LANES
            ].astype(F32)
    buf_cot_ref[...] = wide_cot_ref[...].astype(BF16).reshape(buf_cot_ref.shape)
    stores = [copies.start(buf_cot_ref, send_hbm.at[:, s.block : 2 * s.block])]
    inner_load.wait()
    for r in range(s.rows):
        x_loads[r].wait()
        normed = (x_ref[r].astype(F32) * inv_cols[:, r : r + 1] * gain_ref[...]).astype(BF16)
        y = dot(inner_ref[...], normed, 1, 0) * tw_cols[:, r : r + 1]
        for jh, part, q in s.pieces():
            wide_ref[pl.ds(q + r, s.seq, s.block), :] = y[
                jh * s.seq : (jh + 1) * s.seq, part * LANES : (part + 1) * LANES
            ]
    some = s.seq // CHUNKS
    for k in range(CHUNKS):
        here = slice(k * some, (k + 1) * some)
        wide = wide_ref[k * some * s.block : (k + 1) * some * s.block, :].astype(BF16)
        buf_ref[here] = wide.reshape(some, s.block, LANES)
        stores.append(copies.start(buf_ref.at[here], send_hbm.at[here, 0 : s.block]))
    wait(stores)


def swap_halves(first, second):
    low = lax.broadcasted_iota(jnp.int32, first.shape, 1) < 4
    return (
        jnp.where(low, first, pltpu.roll(second, 4, 1)),
        jnp.where(low, pltpu.roll(first, 4, 1), second),
    )


def unit(n):
    a = lax.broadcasted_iota(jnp.int32, (n, n), 0)
    return jnp.where(a == lax.broadcasted_iota(jnp.int32, (n, n), 1), 1.0, 0.0).astype(BF16)


def sources(s, got_ref, k, tile):
    got = got_ref[k].astype(F32).reshape(s.seq // 2, 2, s.block // 16, 8, LANES)
    return got[:, 0, tile], got[:, 1, tile]


def middle_kernel(
    s, got_hbm, outer_hbm, weight_ref, send_hbm, got_ref, outer_ref, part_ref, out_ref, buf_ref, sems
):
    n1 = s.seq * s.rows
    copies = Copies(sems)
    outer_load = copies.start(outer_hbm, outer_ref)
    loads = {}
    half = s.block // 2
    for k in (0, 2, 1, 3):
        loads[k] = copies.start(got_hbm.at[:, k * half : (k + 1) * half], got_ref.at[k])
    outer_load.wait()
    outer_t = dot(unit(n1), outer_ref[...], 1, 1).astype(BF16)
    for jh in range(s.cols):
        if jh % 2 == 0:
            loads[jh // 2].wait()
            loads[2 + jh // 2].wait()
        rot, cot = (
            jnp.concatenate(
                [v.reshape(n1, LANES) for v in swap_halves(*sources(s, got_ref, k, jh % 2))], axis=1
            ).astype(BF16)
            for k in (jh // 2, 2 + jh // 2)
        )
        v = dot(outer_ref[...], rot, 1, 0).astype(BF16).astype(F32)
        t = jnp.tanh(GELU_C * (v + GELU_A * v * v * v))
        hidden = (0.5 * v * (1.0 + t)).astype(BF16)
        slope = 0.5 * (1.0 + t) + 0.5 * v * (1.0 - t * t) * GELU_C * (1.0 + 3.0 * GELU_A * v * v)
        grad = (dot(cot, weight_ref[...], 1, 1) * slope).astype(BF16)
        product = dot(hidden, cot, 0, 0)
        for part in range(s.parts):
            here = slice(part * s.width, (part + 1) * s.width)
            term = product[:, part * LANES : (part + 1) * LANES]
            part_ref[here, :] = term if jh == 0 else part_ref[here, :] + term
        back = dot(outer_t, grad, 1, 0)
        even, odd = swap_halves(
            back[:, :LANES].reshape(n1 // 8, 8, LANES), back[:, LANES:].reshape(n1 // 8, 8, LANES)
        )
        out_ref[:, 0, jh] = even
        out_ref[:, 1, jh] = odd
    step = s.width // s.seq
    flat = out_ref.reshape(s.seq * (s.block + s.extra), LANES)
    for i in range(step):
        for part in range(s.parts):
            at = s.block + i * s.parts + part
            v = part_ref[pl.ds(part * s.width + i, s.seq, step), :]
            hi = v.astype(BF16).astype(F32)
            flat[pl.ds(at, s.seq, s.block + s.extra), :] = hi
            flat[pl.ds(at + s.extra // 2, s.seq, s.block + s.extra), :] = v - hi
    some = s.seq // CHUNKS
    full = s.block + s.extra
    stores = []
    for k in range(CHUNKS):
        here = slice(k * some, (k + 1) * some)
        buf_ref[here] = flat[k * some * full : (k + 1) * some * full, :].astype(BF16).reshape(some, full, LANES)
        stores.append(copies.start(buf_ref.at[here], send_hbm.at[here]))
    wait(stores)


def back_kernel(
    s, got_hbm, x_hbm, cot_hbm, inner_hbm, inv_ref, gain_ref, tw_ref, sum_hbm, proj_ref,
    got_ref, x_ref, cot_ref, inner_ref, sum_ref, wide_ref, col_ref, sems,
):
    copies = Copies(sems)
    some = s.seq // CHUNKS
    slices = [slice(k * some, (k + 1) * some) for k in range(CHUNKS)]
    got_loads = [copies.start(got_hbm.at[here], got_ref.at[here]) for here in slices]
    inner_load = copies.start(inner_hbm, inner_ref)
    x_loads = copies.rows(x_hbm, x_ref, s.rows)
    cot_loads = copies.rows(cot_hbm, cot_ref, s.rows)
    full = s.block + s.extra
    inv_cols = column_form(inv_ref[...])
    tw_cols = column_form(tw_ref[...])
    for k in range(CHUNKS):
        got_loads[k].wait()
        wide_ref[k * some * full : (k + 1) * some * full, :] = (
            got_ref[slices[k]].astype(F32).reshape(some * full, LANES)
        )
    inner_load.wait()
    inner_t = dot(unit(s.n2), inner_ref[...], 1, 1).astype(BF16)
    stores = []
    for r in range(s.rows):
        for jh, part, q in s.pieces():
            here = slice(jh * s.seq, (jh + 1) * s.seq)
            col_ref[here, part * LANES : (part + 1) * LANES] = (
                wide_ref[pl.ds(q + r, s.seq, full), :] * tw_cols[here, r : r + 1]
            ).astype(BF16)
        grad = dot(inner_t, col_ref[...], 1, 0)
        gained = grad * gain_ref[...]
        x_loads[r].wait()
        proj_ref[r : r + 1, :] = lane_sums(gained * x_ref[r].astype(F32))[0:1]
        cot_loads[r].wait()
        sum_ref[r] = cot_ref[r].astype(F32) + inv_cols[:, r : r + 1] * gained
        stores.append(copies.start(sum_ref.at[r], sum_hbm.at[r]))
    wait(stores)


def finish_kernel(s, sum_hbm, x_hbm, inv_ref, proj_ref, whole_ref, out_hbm, weight_ref, sum_ref, x_ref, out_ref, sems):
    copies = Copies(sems)
    loads = []
    for r in range(s.rows):
        loads.append([copies.start(sum_hbm.at[r], sum_ref.at[r]), copies.start(x_hbm.at[r], x_ref.at[r])])
    inv = inv_ref[...]
    factor = column_form(inv * inv * inv * proj_ref[...] / D)
    stores = []
    for r in range(s.rows):
        wait(loads[r])
        out_ref[r] = (sum_ref[r] - x_ref[r].astype(F32) * factor[:, r : r + 1]).astype(BF16)
        stores.append(copies.start(out_ref.at[r], out_hbm.at[r]))
    for part in range(s.parts):
        weight_ref[:, part * LANES : (part + 1) * LANES] = whole_ref[pl.ds(part, s.width, s.parts), :]
    wait(stores)


def call(kernel, s, name, outs, scratch, copies, flops, moved, far, near):
    hbm, vmem = pl.BlockSpec(memory_space=pl.ANY), pl.BlockSpec(memory_space=pltpu.VMEM)
    return pl.pallas_call(
        functools.partial(kernel, s),
        out_shape=[jax.ShapeDtypeStruct(shape, kind) for shape, kind in outs],
        in_specs=[hbm] * len(far) + [vmem] * len(near),
        out_specs=[hbm if len(shape) == 3 else vmem for shape, _ in outs],
        scratch_shapes=[pltpu.VMEM(shape, kind) for shape, kind in scratch]
        + [pltpu.SemaphoreType.DMA((copies,))],
        compiler_params=pltpu.CompilerParams(vmem_limit_bytes=60 << 20),
        cost_estimate=pl.CostEstimate(flops=flops, bytes_accessed=moved, transcendentals=0),
        name=name,
    )(*far, *near)


def exchange(v):
    return lax.all_to_all(v, "seq", split_axis=0, concat_axis=0, tiled=True)


def on_device(seq, inputs, norm_gain, inner_factor, outer_factor, twiddle, channel_weight, cotangent):
    rows, n2, width = inputs.shape
    s = Sizes(seq, rows, n2, width)
    full = s.block + s.extra
    rows_bf16 = (inputs.shape, BF16)
    square = ((n2, n2), BF16)
    packed = ((seq, s.block, LANES), BF16)
    packed_more = ((seq, full, LANES), BF16)
    wide = ((seq * s.block, LANES), F32)
    small = ((rows, n2), F32)
    mib = rows * n2 * width * 2
    flop = 2 * rows * n2 * n2 * width
    gain = norm_gain.reshape(1, width)

    (part_sum,) = call(square_kernel, s, "squares", [small], [rows_bf16], rows, flop // 20, mib, [inputs], [])
    sq_sum = lax.psum(part_sum, "chan")
    send, inv = call(
        inner_kernel, s, "inner", [((seq, 2 * s.block, LANES), BF16), small],
        [rows_bf16, rows_bf16, square, wide, wide, packed, packed], 2 * rows + 2 + CHUNKS, flop, 5 * mib,
        [inputs, cotangent, inner_factor], [sq_sum, gain, twiddle],
    )
    got = exchange(send)
    (back_send,) = call(
        middle_kernel, s, "middle", [packed_more],
        [
            ((4, seq, s.block // 2, LANES), BF16), (outer_factor.shape, BF16), ((s.parts * width, LANES), F32),
            ((seq // 2, 2, full // 8, 8, LANES), F32), packed_more,
        ],
        5 + CHUNKS, 3 * flop, 4 * mib, [got, outer_factor], [channel_weight[0]],
    )
    back_got = exchange(back_send)
    pairs = jnp.sum(back_got[:, s.block :].astype(F32), axis=0)
    share = pairs[: s.extra // 2] + pairs[s.extra // 2 :]
    whole = exchange(jnp.broadcast_to(share, (seq,) + share.shape))
    base, part_proj = call(
        back_kernel, s, "back", [(inputs.shape, F32), small],
        [packed_more, rows_bf16, rows_bf16, square, (inputs.shape, F32), ((seq * full, LANES), F32), ((n2, width), BF16)],
        CHUNKS + 1 + 3 * rows, flop, 6 * mib, [back_got, inputs, cotangent, inner_factor], [inv, gain, twiddle],
    )
    projection = lax.psum(part_proj, "chan")
    input_grad, weight_grad = call(
        finish_kernel, s, "finish", [rows_bf16, ((width, width), F32)],
        [(inputs.shape, F32), rows_bf16, rows_bf16], 3 * rows, flop // 100, 4 * mib,
        [base, inputs], [inv, projection, whole.reshape(-1, LANES)],
    )
    return (input_grad, weight_grad.reshape(1, width, width))


def solution(mesh):
    in_specs = (
        P("seq", None, "chan"),
        P("chan"),
        P(),
        P(),
        P("seq", None),
        P("chan", None, None),
        P("seq", None, "chan"),
    )
    out_specs = (P("seq", None, "chan"), P("chan", None, None))

    def run(*args):
        return on_device(mesh.shape["seq"], *args)

    return jax.shard_map(run, mesh=mesh, in_specs=in_specs, out_specs=out_specs, check_vma=False)
```

```python
import functools

import jax
import jax.numpy as jnp
from jax import lax
from jax.experimental import pallas as pl
from jax.experimental.pallas import tpu as pltpu
from jax.sharding import PartitionSpec as P

D = 1024
GELU_C = 0.7978845608028654
GELU_A = 0.044715
F32 = jnp.float32
BF16 = jnp.bfloat16
LANES = 128


def dot(a, b, ca, cb):
    return lax.dot_general(a, b, (((ca,), (cb,)), ((), ())), preferred_element_type=F32)


def lane_sums(v):
    ones = jnp.ones((8, v.shape[1]), BF16)
    hi = v.astype(BF16)
    rest = v - hi.astype(F32)
    return dot(ones, hi, 1, 1) + dot(ones, rest.astype(BF16), 1, 1)


def column_form(v):
    r, n = v.shape
    return jnp.concatenate([v] * (8 // r), axis=0).T


class Sizes:
    def __init__(self, seq, rows, n2, width):
        self.seq, self.rows, self.n2, self.width = seq, rows, n2, width
        self.cols = n2 // seq
        self.parts = width // LANES
        self.block = self.cols * self.parts * rows
        self.extra = 2 * (width // seq) * self.parts

    def pieces(self):
        for jh in range(self.cols):
            for part in range(self.parts):
                yield jh, part, (jh * self.parts + part) * self.rows


class Copies:
    def __init__(self, sems):
        self.sems, self.count = sems, 0

    def start(self, source, target):
        copy = pltpu.make_async_copy(source, target, self.sems.at[self.count])
        copy.start()
        self.count += 1
        return copy

    def rows(self, source, target, count):
        return [self.start(source.at[r], target.at[r]) for r in range(count)]


def wait(copies):
    for copy in copies:
        copy.wait()


def square_kernel(s, x_ref, sum_ref):
    for r in range(s.rows):
        x = x_ref[r].astype(F32)
        sum_ref[r : r + 1, :] = lane_sums(x * x)[0:1]


def inner_kernel(
    s, cot_hbm, inner_hbm, x_hbm, gain_hbm, tw_hbm, sum_ref, send_ref, inv_ref,
    cot_ref, inner_ref, x_ref, gain_ref, tw_ref, wide_ref, sems,
):
    copies = Copies(sems)
    cot_load = copies.start(cot_hbm, cot_ref)
    tw_load = copies.start(tw_hbm, tw_ref)
    gain_load = copies.start(gain_hbm, gain_ref)
    inner_load = copies.start(inner_hbm, inner_ref)
    x_load = copies.start(x_hbm, x_ref)
    inv = lax.rsqrt(sum_ref[...] / D + 1e-05)
    inv_ref[...] = inv
    inv_cols = column_form(inv)
    cot_load.wait()
    for r in range(s.rows):
        for jh, part, q in s.pieces():
            wide_ref[pl.ds(s.block + q + r, s.seq, 2 * s.block), :] = cot_ref[
                r, jh * s.seq : (jh + 1) * s.seq, part * LANES : (part + 1) * LANES
            ].astype(F32)
    wait([tw_load, gain_load, inner_load, x_load])
    tw_cols = column_form(tw_ref[...])
    for r in range(s.rows):
        normed = (x_ref[r].astype(F32) * inv_cols[:, r : r + 1] * gain_ref[...]).astype(BF16)
        y = dot(inner_ref[...], normed, 1, 0) * tw_cols[:, r : r + 1]
        for jh, part, q in s.pieces():
            wide_ref[pl.ds(q + r, s.seq, 2 * s.block), :] = y[
                jh * s.seq : (jh + 1) * s.seq, part * LANES : (part + 1) * LANES
            ]
    send_ref[...] = wide_ref[...].astype(BF16)


def swap_halves(first, second):
    low = lax.broadcasted_iota(jnp.int32, first.shape, 1) < 4
    return (
        jnp.where(low, first, pltpu.roll(second, 4, 1)),
        jnp.where(low, pltpu.roll(first, 4, 1), second),
    )


def unit(n):
    a = lax.broadcasted_iota(jnp.int32, (n, n), 0)
    return jnp.where(a == lax.broadcasted_iota(jnp.int32, (n, n), 1), 1.0, 0.0).astype(BF16)


def middle_kernel(s, got_ref, weight_ref, outer_ref, send_ref, part_ref, out_ref):
    n1 = s.seq * s.rows
    outer_t = dot(unit(n1), outer_ref[...], 1, 1).astype(BF16)
    tiles = s.block // 8
    got = got_ref[...].reshape(s.seq // 2, 2, 2 * tiles, 8, LANES)
    for jh in range(s.cols):
        rot, cot = (
            jnp.concatenate(
                [
                    v.reshape(n1, LANES)
                    for v in swap_halves(got[:, 0, tile].astype(F32), got[:, 1, tile].astype(F32))
                ],
                axis=1,
            ).astype(BF16)
            for tile in (jh, tiles + jh)
        )
        v = dot(outer_ref[...], rot, 1, 0).astype(BF16).astype(F32)
        t = jnp.tanh(GELU_C * (v + GELU_A * v * v * v))
        hidden = (0.5 * v * (1.0 + t)).astype(BF16)
        slope = 0.5 * (1.0 + t) + 0.5 * v * (1.0 - t * t) * GELU_C * (1.0 + 3.0 * GELU_A * v * v)
        grad = (dot(cot, weight_ref[...], 1, 1) * slope).astype(BF16)
        product = dot(hidden, cot, 0, 0)
        for part in range(s.parts):
            here = slice(part * s.width, (part + 1) * s.width)
            term = product[:, part * LANES : (part + 1) * LANES]
            part_ref[here, :] = term if jh == 0 else part_ref[here, :] + term
        back = dot(outer_t, grad, 1, 0)
        even, odd = swap_halves(
            back[:, :LANES].reshape(n1 // 8, 8, LANES), back[:, LANES:].reshape(n1 // 8, 8, LANES)
        )
        out_ref[:, 0, jh] = even
        out_ref[:, 1, jh] = odd
    step = s.width // s.seq
    flat = out_ref.reshape(s.seq * (s.block + s.extra), LANES)
    for i in range(step):
        for part in range(s.parts):
            at = s.block + i * s.parts + part
            v = part_ref[pl.ds(part * s.width + i, s.seq, step), :]
            hi = v.astype(BF16).astype(F32)
            flat[pl.ds(at, s.seq, s.block + s.extra), :] = hi
            flat[pl.ds(at + s.extra // 2, s.seq, s.block + s.extra), :] = v - hi
    send_ref[...] = flat[...].astype(BF16)


def back_kernel(
    s, inner_hbm, got_ref, x_ref, cot_ref, inv_ref, gain_ref, tw_ref, sum_hbm, proj_ref,
    inner_ref, sum_ref, wide_ref, col_ref, sems,
):
    copies = Copies(sems)
    load = copies.start(inner_hbm, inner_ref)
    wide_ref[...] = got_ref[...].astype(F32)
    full = s.block + s.extra
    inv_cols = column_form(inv_ref[...])
    tw_cols = column_form(tw_ref[...])
    for r in range(s.rows):
        for jh, part, q in s.pieces():
            here = slice(jh * s.seq, (jh + 1) * s.seq)
            col_ref[r, here, part * LANES : (part + 1) * LANES] = (
                wide_ref[pl.ds(q + r, s.seq, full), :] * tw_cols[here, r : r + 1]
            ).astype(BF16)
    load.wait()
    inner_t = dot(unit(s.n2), inner_ref[...], 1, 1).astype(BF16)
    stores = []
    for r in range(s.rows):
        grad = dot(inner_t, col_ref[r], 1, 0)
        gained = grad * gain_ref[...]
        proj_ref[r : r + 1, :] = lane_sums(gained * x_ref[r].astype(F32))[0:1]
        sum_ref[r] = cot_ref[r].astype(F32) + inv_cols[:, r : r + 1] * gained
        if r % 2 == 1:
            stores.append(copies.start(sum_ref.at[r - 1 : r + 1], sum_hbm.at[r - 1 : r + 1]))
    wait(stores)


def finish_kernel(
    s, sum_hbm, whole_hbm, x_ref, inv_ref, proj_ref, out_hbm, weight_hbm, sum_ref, whole_ref, weight_ref, out_ref, sems
):
    copies = Copies(sems)
    pairs = [slice(r, r + 2) for r in range(0, s.rows, 2)]
    sum_loads = [copies.start(sum_hbm.at[pair], sum_ref.at[pair]) for pair in pairs]
    whole_load = copies.start(whole_hbm, whole_ref)
    inv = inv_ref[...]
    factor = column_form(inv * inv * inv * proj_ref[...] / D)
    stores = []
    for k, pair in enumerate(pairs):
        sum_loads[k].wait()
        for r in (2 * k, 2 * k + 1):
            out_ref[r] = (sum_ref[r] - x_ref[r].astype(F32) * factor[:, r : r + 1]).astype(BF16)
        stores.append(copies.start(out_ref.at[pair], out_hbm.at[pair]))
    whole_load.wait()
    for part in range(s.parts):
        weight_ref[:, part * LANES : (part + 1) * LANES] = whole_ref[pl.ds(part, s.width, s.parts), :]
    stores.append(copies.start(weight_ref, weight_hbm))
    wait(stores)


HBM, AUTO = "hbm", "auto"


def call(kernel, s, name, outs, scratch, copies, flops, moved, *args):
    specs = {AUTO: pl.BlockSpec(memory_space=pltpu.VMEM), HBM: pl.BlockSpec(memory_space=pl.ANY)}
    return pl.pallas_call(
        functools.partial(kernel, s),
        out_shape=[
            (pltpu.HBM if place == HBM else jax.ShapeDtypeStruct)(shape, kind) for shape, kind, place in outs
        ],
        in_specs=[specs[place] for _, place in args],
        out_specs=[specs[place] for _, _, place in outs],
        scratch_shapes=[pltpu.VMEM(shape, kind) for shape, kind in scratch]
        + ([pltpu.SemaphoreType.DMA((copies,))] if copies else []),
        compiler_params=pltpu.CompilerParams(vmem_limit_bytes=24 << 20),
        cost_estimate=pl.CostEstimate(flops=flops, bytes_accessed=moved, transcendentals=0),
        name=name,
    )(*[pltpu.with_memory_space_constraint(v, pltpu.HBM) if place == HBM else v for v, place in args])


def exchange(v, seq):
    packed = v.reshape(seq, -1, LANES)
    return lax.all_to_all(packed, "seq", split_axis=0, concat_axis=0, tiled=True).reshape(v.shape)


def on_device(seq, inputs, norm_gain, inner_factor, outer_factor, twiddle, channel_weight, cotangent):
    rows, n2, width = inputs.shape
    s = Sizes(seq, rows, n2, width)
    packed_two = (2 * seq * s.block, LANES)
    packed_more = (seq * (s.block + s.extra), LANES)
    mib = rows * n2 * width * 2
    flop = 2 * rows * n2 * n2 * width
    gain = norm_gain.reshape(1, width)
    small = (rows, n2)

    (part_sum,) = call(
        square_kernel, s, "squares", [(small, F32, AUTO)], [], 0, flop // 20, mib, (inputs, AUTO)
    )
    sq_sum = lax.psum(part_sum, "chan")
    send, inv = call(
        inner_kernel, s, "inner", [(packed_two, BF16, AUTO), (small, F32, AUTO)],
        [(inputs.shape, BF16), (inner_factor.shape, BF16), (inputs.shape, BF16), (gain.shape, F32), (small, F32), (packed_two, F32)],
        5, flop, 5 * mib,
        (cotangent, HBM), (inner_factor, HBM), (inputs, HBM), (gain, HBM), (twiddle, HBM), (sq_sum, AUTO),
    )
    got = exchange(send, seq)
    (back_send,) = call(
        middle_kernel, s, "middle", [(packed_more, BF16, AUTO)],
        [((s.parts * width, LANES), F32), ((seq // 2, 2, (s.block + s.extra) // 8, 8, LANES), F32)], 0, 3 * flop, 4 * mib,
        (got, AUTO), (channel_weight[0], AUTO), (outer_factor, AUTO),
    )
    back_got = exchange(back_send, seq)
    pairs = back_got.reshape(seq, s.block + s.extra, LANES)[:, s.block :].astype(F32)
    pairs = jnp.sum(pairs, axis=0)
    share = pairs[: s.extra // 2] + pairs[s.extra // 2 :]
    whole = lax.all_to_all(
        jnp.broadcast_to(share, (seq,) + share.shape), "seq", split_axis=0, concat_axis=0, tiled=True
    )
    base, part_proj = call(
        back_kernel, s, "back", [(inputs.shape, F32, HBM), (small, F32, AUTO)],
        [(inner_factor.shape, BF16), (inputs.shape, F32), (packed_more, F32), (inputs.shape, BF16)], 1 + rows // 2, flop, 6 * mib,
        (inner_factor, HBM), (back_got, AUTO), (inputs, AUTO), (cotangent, AUTO), (inv, AUTO), (gain, AUTO), (twiddle, AUTO),
    )
    projection = lax.psum(part_proj, "chan")
    input_grad, weight_grad = call(
        finish_kernel, s, "finish", [(inputs.shape, BF16, HBM), ((width, width), F32, HBM)],
        [(inputs.shape, F32), ((s.parts * width, LANES), F32), ((width, width), F32), (inputs.shape, BF16)],
        rows + 2, flop // 100, 4 * mib,
        (base, HBM), (whole.reshape(-1, LANES), HBM), (inputs, AUTO), (inv, AUTO), (projection, AUTO),
    )
    return (input_grad, weight_grad.reshape(1, width, width))


def solution(mesh):
    in_specs = (
        P("seq", None, "chan"),
        P("chan"),
        P(),
        P(),
        P("seq", None),
        P("chan", None, None),
        P("seq", None, "chan"),
    )
    out_specs = (P("seq", None, "chan"), P("chan", None, None))

    def run(*args):
        return on_device(mesh.shape["seq"], *args)

    return jax.shard_map(run, mesh=mesh, in_specs=in_specs, out_specs=out_specs, check_vma=False)
```

```python
import functools

import jax
import jax.numpy as jnp
from jax import lax
from jax.experimental import pallas as pl
from jax.experimental.pallas import tpu as pltpu
from jax.sharding import PartitionSpec as P

D = 1024
GELU_C = 0.7978845608028654
GELU_A = 0.044715
F32 = jnp.float32
BF16 = jnp.bfloat16
LANES = 128


def dot(a, b, ca, cb):
    return lax.dot_general(a, b, (((ca,), (cb,)), ((), ())), preferred_element_type=F32)


def lane_sums(v):
    ones = jnp.ones((8, v.shape[1]), BF16)
    hi = v.astype(BF16)
    rest = v - hi.astype(F32)
    return dot(ones, hi, 1, 1) + dot(ones, rest.astype(BF16), 1, 1)


def column_form(v):
    r, n = v.shape
    return jnp.concatenate([v] * (8 // r), axis=0).T


class Sizes:
    def __init__(self, seq, rows, n2, width):
        self.seq, self.rows, self.n2, self.width = seq, rows, n2, width
        self.cols = n2 // seq
        self.parts = width // LANES
        self.block = self.cols * self.parts * rows
        self.extra = 2 * (width // seq) * self.parts

    def pieces(self):
        for jh in range(self.cols):
            for part in range(self.parts):
                yield jh, part, (jh * self.parts + part) * self.rows


def total(ref):
    terms = [ref[k] for k in range(ref.shape[0])]
    while len(terms) > 1:
        terms = [a + b for a, b in zip(terms[::2], terms[1::2])]
    return terms[0]


class Copies:
    def __init__(self, sems):
        self.sems, self.count = sems, 0

    def start(self, source, target):
        copy = pltpu.make_async_copy(source, target, self.sems.at[self.count])
        copy.start()
        self.count += 1
        return copy

    def rows(self, source, target, count):
        return [self.start(source.at[r], target.at[r]) for r in range(count)]


def wait(copies):
    for copy in copies:
        copy.wait()


def square_kernel(s, x_ref, sum_ref):
    for r in range(s.rows):
        x = x_ref[r].astype(F32)
        sum_ref[r : r + 1, :] = lane_sums(x * x)[0:1]


def inner_kernel(
    s, cot_hbm, inner_hbm, x_hbm, gain_hbm, tw_hbm, sum_ref, send_ref, inv_ref,
    cot_ref, inner_ref, x_ref, gain_ref, tw_ref, wide_ref, sems,
):
    copies = Copies(sems)
    pairs = [slice(r, r + 2) for r in range(0, s.rows, 2)]
    cot_loads = [copies.start(cot_hbm.at[pair], cot_ref.at[pair]) for pair in pairs]
    tw_load = copies.start(tw_hbm, tw_ref)
    gain_load = copies.start(gain_hbm, gain_ref)
    inner_load = copies.start(inner_hbm, inner_ref)
    x_load = copies.start(x_hbm, x_ref)
    inv = lax.rsqrt(total(sum_ref) / D + 1e-05)
    inv_ref[...] = inv
    inv_cols = column_form(inv)
    for r in range(s.rows):
        if r % 2 == 0:
            cot_loads[r // 2].wait()
        for jh, part, q in s.pieces():
            wide_ref[pl.ds(s.block + q + r, s.seq, 2 * s.block), :] = cot_ref[
                r, jh * s.seq : (jh + 1) * s.seq, part * LANES : (part + 1) * LANES
            ].astype(F32)
    wait([tw_load, gain_load, inner_load, x_load])
    tw_cols = column_form(tw_ref[...])
    for r in range(s.rows):
        normed = (x_ref[r].astype(F32) * inv_cols[:, r : r + 1] * gain_ref[...]).astype(BF16)
        y = dot(inner_ref[...], normed, 1, 0) * tw_cols[:, r : r + 1]
        for jh, part, q in s.pieces():
            wide_ref[pl.ds(q + r, s.seq, 2 * s.block), :] = y[
                jh * s.seq : (jh + 1) * s.seq, part * LANES : (part + 1) * LANES
            ]
    send_ref[...] = wide_ref[...].astype(BF16)


def swap_halves(first, second):
    low = lax.broadcasted_iota(jnp.int32, first.shape, 1) < 4
    return (
        jnp.where(low, first, pltpu.roll(second, 4, 1)),
        jnp.where(low, pltpu.roll(first, 4, 1), second),
    )


def unit(n):
    a = lax.broadcasted_iota(jnp.int32, (n, n), 0)
    return jnp.where(a == lax.broadcasted_iota(jnp.int32, (n, n), 1), 1.0, 0.0).astype(BF16)


def middle_kernel(s, got_ref, weight_ref, outer_ref, send_ref, part_ref, out_ref):
    n1 = s.seq * s.rows
    outer_t = dot(unit(n1), outer_ref[...], 1, 1).astype(BF16)
    tiles = s.block // 8
    got = got_ref[...].reshape(s.seq // 2, 2, 2 * tiles, 8, LANES)
    for jh in range(s.cols):
        rot, cot = (
            jnp.concatenate(
                [
                    v.reshape(n1, LANES)
                    for v in swap_halves(got[:, 0, tile].astype(F32), got[:, 1, tile].astype(F32))
                ],
                axis=1,
            ).astype(BF16)
            for tile in (jh, tiles + jh)
        )
        v = dot(outer_ref[...], rot, 1, 0).astype(BF16).astype(F32)
        t = jnp.tanh(GELU_C * (v + GELU_A * v * v * v))
        hidden = (0.5 * v * (1.0 + t)).astype(BF16)
        slope = 0.5 * (1.0 + t) + 0.5 * v * (1.0 - t * t) * GELU_C * (1.0 + 3.0 * GELU_A * v * v)
        grad = (dot(cot, weight_ref[...], 1, 1) * slope).astype(BF16)
        product = dot(hidden, cot, 0, 0)
        for part in range(s.parts):
            here = slice(part * s.width, (part + 1) * s.width)
            term = product[:, part * LANES : (part + 1) * LANES]
            part_ref[here, :] = term if jh == 0 else part_ref[here, :] + term
        back = dot(outer_t, grad, 1, 0)
        even, odd = swap_halves(
            back[:, :LANES].reshape(n1 // 8, 8, LANES), back[:, LANES:].reshape(n1 // 8, 8, LANES)
        )
        out_ref[:, 0, jh] = even
        out_ref[:, 1, jh] = odd
    step = s.width // s.seq
    flat = out_ref.reshape(s.seq * (s.block + s.extra), LANES)
    for i in range(step):
        for part in range(s.parts):
            at = s.block + i * s.parts + part
            v = part_ref[pl.ds(part * s.width + i, s.seq, step), :]
            hi = v.astype(BF16).astype(F32)
            flat[pl.ds(at, s.seq, s.block + s.extra), :] = hi
            flat[pl.ds(at + s.extra // 2, s.seq, s.block + s.extra), :] = v - hi
    send_ref[...] = flat[...].astype(BF16)


def back_kernel(
    s, inner_hbm, got_ref, x_ref, cot_ref, inv_ref, gain_ref, tw_ref, sum_hbm, proj_ref,
    inner_ref, sum_ref, wide_ref, col_ref, sems,
):
    copies = Copies(sems)
    load = copies.start(inner_hbm, inner_ref)
    wide_ref[...] = got_ref[...].astype(F32)
    full = s.block + s.extra
    inv_cols = column_form(inv_ref[...])
    tw_cols = column_form(tw_ref[...])
    for r in range(s.rows):
        for jh, part, q in s.pieces():
            here = slice(jh * s.seq, (jh + 1) * s.seq)
            col_ref[r, here, part * LANES : (part + 1) * LANES] = (
                wide_ref[pl.ds(q + r, s.seq, full), :] * tw_cols[here, r : r + 1]
            ).astype(BF16)
    load.wait()
    inner_t = dot(unit(s.n2), inner_ref[...], 1, 1).astype(BF16)
    stores = []
    for r in range(s.rows):
        grad = dot(inner_t, col_ref[r], 1, 0)
        gained = grad * gain_ref[...]
        proj_ref[r : r + 1, :] = lane_sums(gained * x_ref[r].astype(F32))[0:1]
        sum_ref[r] = cot_ref[r].astype(F32) + inv_cols[:, r : r + 1] * gained
        stores.append(copies.start(sum_ref.at[r], sum_hbm.at[r]))
    wait(stores)


def finish_kernel(
    s, sum_hbm, whole_hbm, x_ref, inv_ref, proj_ref, out_hbm, weight_hbm, sum_ref, whole_ref, weight_ref, out_ref, sems
):
    copies = Copies(sems)
    sum_loads = [copies.start(sum_hbm.at[r], sum_ref.at[r]) for r in range(s.rows)]
    whole_load = copies.start(whole_hbm, whole_ref)
    inv = inv_ref[...]
    factor = column_form(inv * inv * inv * total(proj_ref) / D)
    stores = []
    for r in range(s.rows):
        sum_loads[r].wait()
        out_ref[r] = (sum_ref[r] - x_ref[r].astype(F32) * factor[:, r : r + 1]).astype(BF16)
        if r % 2 == 1:
            stores.append(copies.start(out_ref.at[r - 1 : r + 1], out_hbm.at[r - 1 : r + 1]))
    whole_load.wait()
    for part in range(s.parts):
        weight_ref[:, part * LANES : (part + 1) * LANES] = whole_ref[pl.ds(part, s.width, s.parts), :]
    stores.append(copies.start(weight_ref, weight_hbm))
    wait(stores)


HBM, AUTO = "hbm", "auto"


def call(kernel, s, name, outs, scratch, copies, flops, moved, *args):
    specs = {AUTO: pl.BlockSpec(memory_space=pltpu.VMEM), HBM: pl.BlockSpec(memory_space=pl.ANY)}
    return pl.pallas_call(
        functools.partial(kernel, s),
        out_shape=[
            (pltpu.HBM if place == HBM else jax.ShapeDtypeStruct)(shape, kind) for shape, kind, place in outs
        ],
        in_specs=[specs[place] for _, place in args],
        out_specs=[specs[place] for _, _, place in outs],
        scratch_shapes=[pltpu.VMEM(shape, kind) for shape, kind in scratch]
        + ([pltpu.SemaphoreType.DMA((copies,))] if copies else []),
        compiler_params=pltpu.CompilerParams(vmem_limit_bytes=24 << 20),
        cost_estimate=pl.CostEstimate(flops=flops, bytes_accessed=moved, transcendentals=0),
        name=name,
    )(*[pltpu.with_memory_space_constraint(v, pltpu.HBM) if place == HBM else v for v, place in args])


def exchange(v, seq):
    packed = v.reshape(seq, -1, LANES)
    return lax.all_to_all(packed, "seq", split_axis=0, concat_axis=0, tiled=True).reshape(v.shape)


def on_device(seq, inputs, norm_gain, inner_factor, outer_factor, twiddle, channel_weight, cotangent):
    rows, n2, width = inputs.shape
    s = Sizes(seq, rows, n2, width)
    packed_two = (2 * seq * s.block, LANES)
    packed_more = (seq * (s.block + s.extra), LANES)
    mib = rows * n2 * width * 2
    flop = 2 * rows * n2 * n2 * width
    gain = norm_gain.reshape(1, width)
    small = (rows, n2)

    (part_sum,) = call(
        square_kernel, s, "squares", [(small, F32, AUTO)], [], 0, flop // 20, mib, (inputs, AUTO)
    )
    sums = lax.all_gather(part_sum, "chan")
    send, inv = call(
        inner_kernel, s, "inner", [(packed_two, BF16, AUTO), (small, F32, AUTO)],
        [(inputs.shape, BF16), (inner_factor.shape, BF16), (inputs.shape, BF16), (gain.shape, F32), (small, F32), (packed_two, F32)],
        4 + rows // 2, flop, 5 * mib,
        (cotangent, HBM), (inner_factor, HBM), (inputs, HBM), (gain, HBM), (twiddle, HBM), (sums, AUTO),
    )
    got = exchange(send, seq)
    (back_send,) = call(
        middle_kernel, s, "middle", [(packed_more, BF16, AUTO)],
        [((s.parts * width, LANES), F32), ((seq // 2, 2, (s.block + s.extra) // 8, 8, LANES), F32)], 0, 3 * flop, 4 * mib,
        (got, AUTO), (channel_weight[0], AUTO), (outer_factor, AUTO),
    )
    back_got = exchange(back_send, seq)
    pairs = back_got.reshape(seq, s.block + s.extra, LANES)[:, s.block :].astype(F32)
    pairs = jnp.sum(pairs, axis=0)
    share = pairs[: s.extra // 2] + pairs[s.extra // 2 :]
    whole = lax.all_to_all(
        jnp.broadcast_to(share, (seq,) + share.shape), "seq", split_axis=0, concat_axis=0, tiled=True
    )
    base, part_proj = call(
        back_kernel, s, "back", [(inputs.shape, F32, HBM), (small, F32, AUTO)],
        [(inner_factor.shape, BF16), (inputs.shape, F32), (packed_more, F32), (inputs.shape, BF16)], 1 + rows, flop, 6 * mib,
        (inner_factor, HBM), (back_got, AUTO), (inputs, AUTO), (cotangent, AUTO), (inv, AUTO), (gain, AUTO), (twiddle, AUTO),
    )
    projections = lax.all_gather(part_proj, "chan")
    input_grad, weight_grad = call(
        finish_kernel, s, "finish", [(inputs.shape, BF16, HBM), ((width, width), F32, HBM)],
        [(inputs.shape, F32), ((s.parts * width, LANES), F32), ((width, width), F32), (inputs.shape, BF16)],
        rows + rows // 2 + 2, flop // 100, 4 * mib,
        (base, HBM), (whole.reshape(-1, LANES), HBM), (inputs, AUTO), (inv, AUTO), (projections, AUTO),
    )
    return (input_grad, weight_grad.reshape(1, width, width))


def solution(mesh):
    in_specs = (
        P("seq", None, "chan"),
        P("chan"),
        P(),
        P(),
        P("seq", None),
        P("chan", None, None),
        P("seq", None, "chan"),
    )
    out_specs = (P("seq", None, "chan"), P("chan", None, None))

    def run(*args):
        return on_device(mesh.shape["seq"], *args)

    return jax.shard_map(run, mesh=mesh, in_specs=in_specs, out_specs=out_specs, check_vma=False)
```

```python
import functools

import jax
import jax.numpy as jnp
from jax import lax
from jax.experimental import pallas as pl
from jax.experimental.pallas import tpu as pltpu
from jax.sharding import PartitionSpec as P

D = 1024
GELU_C = 0.7978845608028654
GELU_A = 0.044715
F32 = jnp.float32
BF16 = jnp.bfloat16
LANES = 128


def dot(a, b, ca, cb):
    return lax.dot_general(a, b, (((ca,), (cb,)), ((), ())), preferred_element_type=F32)


def lane_sums(v):
    ones = jnp.ones((8, v.shape[1]), BF16)
    hi = v.astype(BF16)
    rest = v - hi.astype(F32)
    return dot(ones, hi, 1, 1) + dot(ones, rest.astype(BF16), 1, 1)


def column_form(v):
    r, n = v.shape
    return jnp.concatenate([v] * (8 // r), axis=0).T


class Sizes:
    def __init__(self, seq, rows, n2, width):
        self.seq, self.rows, self.n2, self.width = seq, rows, n2, width
        self.cols = n2 // seq
        self.parts = width // LANES
        self.block = self.cols * self.parts * rows

    def pieces(self):
        for jh in range(self.cols):
            for part in range(self.parts):
                yield jh, part, (jh * self.parts + part) * self.rows


def total(ref):
    terms = [ref[k] for k in range(ref.shape[0])]
    while len(terms) > 1:
        terms = [a + b for a, b in zip(terms[::2], terms[1::2])]
    return terms[0]


class Copies:
    def __init__(self, sems):
        self.sems, self.count = sems, 0

    def start(self, source, target):
        copy = pltpu.make_async_copy(source, target, self.sems.at[self.count])
        copy.start()
        self.count += 1
        return copy

    def rows(self, source, target, count):
        return [self.start(source.at[r], target.at[r]) for r in range(count)]


def wait(copies):
    for copy in copies:
        copy.wait()


def square_kernel(s, x_ref, sum_ref):
    for r in range(s.rows):
        x = x_ref[r].astype(F32)
        sum_ref[r : r + 1, :] = lane_sums(x * x)[0:1]


def inner_kernel(
    s, cot_hbm, inner_hbm, x_hbm, gain_hbm, tw_hbm, sum_ref, send_ref, inv_ref,
    cot_ref, inner_ref, x_ref, gain_ref, tw_ref, wide_ref, sems,
):
    copies = Copies(sems)
    pairs = [slice(r, r + 2) for r in range(0, s.rows, 2)]
    cot_loads = [copies.start(cot_hbm.at[pair], cot_ref.at[pair]) for pair in pairs]
    tw_load = copies.start(tw_hbm, tw_ref)
    gain_load = copies.start(gain_hbm, gain_ref)
    inner_load = copies.start(inner_hbm, inner_ref)
    x_load = copies.start(x_hbm, x_ref)
    inv = lax.rsqrt(total(sum_ref) / D + 1e-05)
    inv_ref[...] = inv
    inv_cols = column_form(inv)
    for r in range(s.rows):
        if r % 2 == 0:
            cot_loads[r // 2].wait()
        for jh, part, q in s.pieces():
            wide_ref[pl.ds(s.block + q + r, s.seq, 2 * s.block), :] = cot_ref[
                r, jh * s.seq : (jh + 1) * s.seq, part * LANES : (part + 1) * LANES
            ].astype(F32)
    wait([tw_load, gain_load, inner_load, x_load])
    tw_cols = column_form(tw_ref[...])
    for r in range(s.rows):
        normed = (x_ref[r].astype(F32) * inv_cols[:, r : r + 1] * gain_ref[...]).astype(BF16)
        y = dot(inner_ref[...], normed, 1, 0) * tw_cols[:, r : r + 1]
        for jh, part, q in s.pieces():
            wide_ref[pl.ds(q + r, s.seq, 2 * s.block), :] = y[
                jh * s.seq : (jh + 1) * s.seq, part * LANES : (part + 1) * LANES
            ]
    send_ref[...] = wide_ref[...].astype(BF16)


def swap_halves(first, second):
    low = lax.broadcasted_iota(jnp.int32, first.shape, 1) < 4
    return (
        jnp.where(low, first, pltpu.roll(second, 4, 1)),
        jnp.where(low, pltpu.roll(first, 4, 1), second),
    )


def unit(n):
    a = lax.broadcasted_iota(jnp.int32, (n, n), 0)
    return jnp.where(a == lax.broadcasted_iota(jnp.int32, (n, n), 1), 1.0, 0.0).astype(BF16)


def put(out_ref, q, v):
    v = v.reshape(-1, 8, LANES)
    out_ref[:, 0, q] = v[:, :4]
    out_ref[:, 1, q] = v[:, 4:]


def middle_kernel(s, got_ref, weight_ref, outer_ref, send_ref, part_ref, out_ref, piece_ref):
    n1 = s.seq * s.rows
    outer_t = dot(unit(n1), outer_ref[...], 1, 1).astype(BF16)
    tiles = s.block // 8
    got = got_ref[...].reshape(s.seq // 2, 2, 2 * tiles, 8, LANES)
    for jh in range(s.cols):
        rot, cot = (
            jnp.concatenate(
                [
                    v.reshape(n1, LANES)
                    for v in swap_halves(got[:, 0, tile].astype(F32), got[:, 1, tile].astype(F32))
                ],
                axis=1,
            ).astype(BF16)
            for tile in (jh, tiles + jh)
        )
        v = dot(outer_ref[...], rot, 1, 0).astype(BF16).astype(F32)
        t = jnp.tanh(GELU_C * (v + GELU_A * v * v * v))
        hidden = (0.5 * v * (1.0 + t)).astype(BF16)
        slope = 0.5 * (1.0 + t) + 0.5 * v * (1.0 - t * t) * GELU_C * (1.0 + 3.0 * GELU_A * v * v)
        grad = (dot(cot, weight_ref[...], 1, 1) * slope).astype(BF16)
        product = dot(hidden, cot, 0, 0)
        for part in range(s.parts):
            here = slice(part * s.width, (part + 1) * s.width)
            term = product[:, part * LANES : (part + 1) * LANES]
            part_ref[here, :] = term if jh == 0 else part_ref[here, :] + term
        back = dot(outer_t, grad, 1, 0)
        for part in range(s.parts):
            put(out_ref, jh * s.parts + part, back[:, part * LANES : (part + 1) * LANES])
    step = s.width // s.seq
    for i in range(step):
        for part in range(s.parts):
            piece_ref[pl.ds(i * s.parts + part, s.seq, step * s.parts), :] = part_ref[
                pl.ds(part * s.width + i, s.seq, step), :
            ]
    put(out_ref, s.cols * s.parts, piece_ref[...])
    send_ref[...] = out_ref[...].astype(BF16)


def back_kernel(
    s, inner_hbm, got_ref, x_ref, cot_ref, inv_ref, gain_ref, tw_ref, sum_hbm, proj_ref,
    inner_ref, sum_ref, wide_ref, col_ref, sems,
):
    copies = Copies(sems)
    load = copies.start(inner_hbm, inner_ref)
    tiles = wide_ref.reshape(s.seq, s.block // 8, 8, LANES)
    for p in range(s.block // 8):
        both = [got_ref[:, :, q].astype(F32) for q in (2 * p, 2 * p + 1)]
        tiles[:, p] = jnp.concatenate(both, axis=2).reshape(s.seq, 8, LANES)
    inv_cols = column_form(inv_ref[...])
    tw_cols = column_form(tw_ref[...])
    for r in range(s.rows):
        for jh, part, q in s.pieces():
            here = slice(jh * s.seq, (jh + 1) * s.seq)
            col_ref[r, here, part * LANES : (part + 1) * LANES] = (
                wide_ref[pl.ds(q + r, s.seq, s.block), :] * tw_cols[here, r : r + 1]
            ).astype(BF16)
    load.wait()
    inner_t = dot(unit(s.n2), inner_ref[...], 1, 1).astype(BF16)
    stores = []
    for r in range(s.rows):
        grad = dot(inner_t, col_ref[r], 1, 0)
        gained = grad * gain_ref[...]
        proj_ref[r : r + 1, :] = lane_sums(gained * x_ref[r].astype(F32))[0:1]
        sum_ref[r] = cot_ref[r].astype(F32) + inv_cols[:, r : r + 1] * gained
        stores.append(copies.start(sum_ref.at[r], sum_hbm.at[r]))
    wait(stores)


def finish_kernel(
    s, sum_hbm, whole_hbm, x_ref, inv_ref, proj_ref, out_hbm, weight_hbm, sum_ref, whole_ref, weight_ref, out_ref, sems
):
    copies = Copies(sems)
    sum_loads = [copies.start(sum_hbm.at[r], sum_ref.at[r]) for r in range(s.rows)]
    whole_load = copies.start(whole_hbm, whole_ref)
    inv = inv_ref[...]
    factor = column_form(inv * inv * inv * total(proj_ref) / D)
    stores = []
    for r in range(s.rows):
        sum_loads[r].wait()
        out_ref[r] = (sum_ref[r] - x_ref[r].astype(F32) * factor[:, r : r + 1]).astype(BF16)
        if r % 2 == 1:
            stores.append(copies.start(out_ref.at[r - 1 : r + 1], out_hbm.at[r - 1 : r + 1]))
    whole_load.wait()
    for part in range(s.parts):
        weight_ref[:, part * LANES : (part + 1) * LANES] = whole_ref[pl.ds(part, s.width, s.parts), :]
    stores.append(copies.start(weight_ref, weight_hbm))
    wait(stores)


HBM, AUTO = "hbm", "auto"


def call(kernel, s, name, outs, scratch, copies, flops, moved, *args):
    specs = {AUTO: pl.BlockSpec(memory_space=pltpu.VMEM), HBM: pl.BlockSpec(memory_space=pl.ANY)}
    return pl.pallas_call(
        functools.partial(kernel, s),
        out_shape=[
            (pltpu.HBM if place == HBM else jax.ShapeDtypeStruct)(shape, kind) for shape, kind, place in outs
        ],
        in_specs=[specs[place] for _, place in args],
        out_specs=[specs[place] for _, _, place in outs],
        scratch_shapes=[pltpu.VMEM(shape, kind) for shape, kind in scratch]
        + ([pltpu.SemaphoreType.DMA((copies,))] if copies else []),
        compiler_params=pltpu.CompilerParams(vmem_limit_bytes=24 << 20),
        cost_estimate=pl.CostEstimate(flops=flops, bytes_accessed=moved, transcendentals=0),
        name=name,
    )(*[pltpu.with_memory_space_constraint(v, pltpu.HBM) if place == HBM else v for v, place in args])


def exchange(v, seq):
    packed = v.reshape(seq, -1, LANES)
    return lax.all_to_all(packed, "seq", split_axis=0, concat_axis=0, tiled=True).reshape(v.shape)


def on_device(seq, inputs, norm_gain, inner_factor, outer_factor, twiddle, channel_weight, cotangent):
    rows, n2, width = inputs.shape
    s = Sizes(seq, rows, n2, width)
    packed_two = (2 * seq * s.block, LANES)
    groups = s.cols * s.parts + 1
    sent = (seq // 2, 2, groups, rows, LANES)
    mib = rows * n2 * width * 2
    flop = 2 * rows * n2 * n2 * width
    gain = norm_gain.reshape(1, width)
    small = (rows, n2)

    (part_sum,) = call(
        square_kernel, s, "squares", [(small, F32, AUTO)], [], 0, flop // 20, mib, (inputs, AUTO)
    )
    sums = lax.all_gather(part_sum, "chan")
    send, inv = call(
        inner_kernel, s, "inner", [(packed_two, BF16, AUTO), (small, F32, AUTO)],
        [(inputs.shape, BF16), (inner_factor.shape, BF16), (inputs.shape, BF16), (gain.shape, F32), (small, F32), (packed_two, F32)],
        4 + rows // 2, flop, 5 * mib,
        (cotangent, HBM), (inner_factor, HBM), (inputs, HBM), (gain, HBM), (twiddle, HBM), (sums, AUTO),
    )
    got = exchange(send, seq)
    (back_send,) = call(
        middle_kernel, s, "middle", [(sent, BF16, AUTO)],
        [((s.parts * width, LANES), F32), (sent, F32), ((rows * seq, LANES), F32)], 0, 3 * flop, 4 * mib,
        (got, AUTO), (channel_weight[0], AUTO), (outer_factor, AUTO),
    )
    back_got = lax.all_to_all(
        back_send.reshape(seq * groups, rows, LANES), "seq", split_axis=0, concat_axis=0, tiled=True
    ).reshape(sent)
    share = jnp.sum(back_got[:, :, -1].astype(F32), axis=(0, 1))
    whole = lax.all_to_all(
        jnp.broadcast_to(share, (seq,) + share.shape), "seq", split_axis=0, concat_axis=0, tiled=True
    )
    base, part_proj = call(
        back_kernel, s, "back", [(inputs.shape, F32, HBM), (small, F32, AUTO)],
        [(inner_factor.shape, BF16), (inputs.shape, F32), ((seq * s.block, LANES), F32), (inputs.shape, BF16)], 1 + rows, flop, 6 * mib,
        (inner_factor, HBM), (back_got, AUTO), (inputs, AUTO), (cotangent, AUTO), (inv, AUTO), (gain, AUTO), (twiddle, AUTO),
    )
    projections = lax.all_gather(part_proj, "chan")
    input_grad, weight_grad = call(
        finish_kernel, s, "finish", [(inputs.shape, BF16, HBM), ((width, width), F32, HBM)],
        [(inputs.shape, F32), ((s.parts * width, LANES), F32), ((width, width), F32), (inputs.shape, BF16)],
        rows + rows // 2 + 2, flop // 100, 4 * mib,
        (base, HBM), (whole.reshape(-1, LANES), HBM), (inputs, AUTO), (inv, AUTO), (projections, AUTO),
    )
    return (input_grad, weight_grad.reshape(1, width, width))


def solution(mesh):
    in_specs = (
        P("seq", None, "chan"),
        P("chan"),
        P(),
        P(),
        P("seq", None),
        P("chan", None, None),
        P("seq", None, "chan"),
    )
    out_specs = (P("seq", None, "chan"), P("chan", None, None))

    def run(*args):
        return on_device(mesh.shape["seq"], *args)

    return jax.shard_map(run, mesh=mesh, in_specs=in_specs, out_specs=out_specs, check_vma=False)
```

```python
import functools

import jax
import jax.numpy as jnp
from jax import lax
from jax.experimental import pallas as pl
from jax.experimental.pallas import tpu as pltpu
from jax.sharding import PartitionSpec as P

D = 1024
GELU_C = 0.7978845608028654
GELU_A = 0.044715
F32 = jnp.float32
BF16 = jnp.bfloat16
LANES = 128


def dot(a, b, ca, cb):
    return lax.dot_general(a, b, (((ca,), (cb,)), ((), ())), preferred_element_type=F32)


def lane_sums(v):
    ones = jnp.ones((8, v.shape[1]), BF16)
    hi = v.astype(BF16)
    rest = v - hi.astype(F32)
    return dot(ones, hi, 1, 1) + dot(ones, rest.astype(BF16), 1, 1)


def column_form(v):
    r, n = v.shape
    return jnp.concatenate([v] * (8 // r), axis=0).T


class Sizes:
    def __init__(self, seq, rows, n2, width):
        self.seq, self.rows, self.n2, self.width = seq, rows, n2, width
        self.cols = n2 // seq
        self.parts = width // LANES
        self.block = self.cols * self.parts * rows

    def pieces(self):
        for jh in range(self.cols):
            for part in range(self.parts):
                yield jh, part, (jh * self.parts + part) * self.rows


def total(ref):
    terms = [ref[k] for k in range(ref.shape[0])]
    while len(terms) > 1:
        terms = [a + b for a, b in zip(terms[::2], terms[1::2])]
    return terms[0]


class Copies:
    def __init__(self, sems):
        self.sems, self.count = sems, 0

    def start(self, source, target):
        copy = pltpu.make_async_copy(source, target, self.sems.at[self.count])
        copy.start()
        self.count += 1
        return copy

    def rows(self, source, target, count):
        return [self.start(source.at[r], target.at[r]) for r in range(count)]


def wait(copies):
    for copy in copies:
        copy.wait()


def square_kernel(s, x_ref, sum_ref):
    for r in range(s.rows):
        x = x_ref[r].astype(F32)
        sum_ref[r : r + 1, :] = lane_sums(x * x)[0:1]


def inner_kernel(
    s, cot_hbm, inner_hbm, x_hbm, gain_hbm, tw_hbm, sum_ref, send_ref, inv_ref,
    cot_ref, inner_ref, x_ref, gain_ref, tw_ref, wide_ref, sems,
):
    copies = Copies(sems)
    cot_loads = [copies.start(cot_hbm.at[r], cot_ref.at[r]) for r in range(s.rows)]
    tw_load = copies.start(tw_hbm, tw_ref)
    gain_load = copies.start(gain_hbm, gain_ref)
    inner_load = copies.start(inner_hbm, inner_ref)
    x_load = copies.start(x_hbm, x_ref)
    inv = lax.rsqrt(total(sum_ref) / D + 1e-05)
    inv_ref[...] = inv
    inv_cols = column_form(inv)
    for r in range(s.rows):
        cot_loads[r].wait()
        for jh, part, q in s.pieces():
            wide_ref[pl.ds(s.block + q + r, s.seq, 2 * s.block), :] = cot_ref[
                r, jh * s.seq : (jh + 1) * s.seq, part * LANES : (part + 1) * LANES
            ].astype(F32)
    wait([tw_load, gain_load, inner_load, x_load])
    tw_cols = column_form(tw_ref[...])
    for r in range(s.rows):
        normed = (x_ref[r].astype(F32) * inv_cols[:, r : r + 1] * gain_ref[...]).astype(BF16)
        y = dot(inner_ref[...], normed, 1, 0) * tw_cols[:, r : r + 1]
        for jh, part, q in s.pieces():
            wide_ref[pl.ds(q + r, s.seq, 2 * s.block), :] = y[
                jh * s.seq : (jh + 1) * s.seq, part * LANES : (part + 1) * LANES
            ]
    send_ref[...] = wide_ref[...].astype(BF16)


def swap_halves(first, second):
    low = lax.broadcasted_iota(jnp.int32, first.shape, 1) < 4
    return (
        jnp.where(low, first, pltpu.roll(second, 4, 1)),
        jnp.where(low, pltpu.roll(first, 4, 1), second),
    )


def unit(n):
    a = lax.broadcasted_iota(jnp.int32, (n, n), 0)
    return jnp.where(a == lax.broadcasted_iota(jnp.int32, (n, n), 1), 1.0, 0.0).astype(BF16)


def put(out_ref, q, v):
    v = v.reshape(-1, 8, LANES)
    out_ref[:, 0, q] = v[:, :4].astype(BF16)
    out_ref[:, 1, q] = v[:, 4:].astype(BF16)


def middle_kernel(s, got_ref, weight_ref, outer_ref, send_ref, part_ref, piece_ref):
    n1 = s.seq * s.rows
    outer_t = dot(unit(n1), outer_ref[...], 1, 1).astype(BF16)
    tiles = s.block // 8
    got = got_ref[...].reshape(s.seq // 2, 2, 2 * tiles, 8, LANES)
    for jh in range(s.cols):
        rot, cot = (
            jnp.concatenate(
                [
                    v.reshape(n1, LANES)
                    for v in swap_halves(got[:, 0, tile].astype(F32), got[:, 1, tile].astype(F32))
                ],
                axis=1,
            ).astype(BF16)
            for tile in (jh, tiles + jh)
        )
        v = dot(outer_ref[...], rot, 1, 0).astype(BF16).astype(F32)
        t = jnp.tanh(GELU_C * (v + GELU_A * v * v * v))
        hidden = (0.5 * v * (1.0 + t)).astype(BF16)
        slope = 0.5 * (1.0 + t) + 0.5 * v * (1.0 - t * t) * GELU_C * (1.0 + 3.0 * GELU_A * v * v)
        grad = (dot(cot, weight_ref[...], 1, 1) * slope).astype(BF16)
        product = dot(hidden, cot, 0, 0)
        for part in range(s.parts):
            here = slice(part * s.width, (part + 1) * s.width)
            term = product[:, part * LANES : (part + 1) * LANES]
            part_ref[here, :] = term if jh == 0 else part_ref[here, :] + term
        back = dot(outer_t, grad, 1, 0)
        for part in range(s.parts):
            put(send_ref, jh * s.parts + part, back[:, part * LANES : (part + 1) * LANES])
    step = s.width // s.seq
    for i in range(step):
        for part in range(s.parts):
            piece_ref[pl.ds(i * s.parts + part, s.seq, step * s.parts), :] = part_ref[
                pl.ds(part * s.width + i, s.seq, step), :
            ]
    put(send_ref, s.cols * s.parts, piece_ref[...])


def back_kernel(
    s, inner_hbm, got_ref, x_ref, cot_ref, inv_ref, gain_ref, tw_ref, sum_hbm, proj_ref,
    inner_ref, sum_ref, wide_ref, col_ref, sems,
):
    copies = Copies(sems)
    load = copies.start(inner_hbm, inner_ref)
    tiles = wide_ref.reshape(s.seq, s.block // 8, 8, LANES)
    for p in range(s.block // 8):
        both = [got_ref[:, :, q].astype(F32) for q in (2 * p, 2 * p + 1)]
        tiles[:, p] = jnp.concatenate(both, axis=2).reshape(s.seq, 8, LANES)
    inv_cols = column_form(inv_ref[...])
    tw_cols = column_form(tw_ref[...])
    for r in range(s.rows):
        for jh, part, q in s.pieces():
            here = slice(jh * s.seq, (jh + 1) * s.seq)
            col_ref[r, here, part * LANES : (part + 1) * LANES] = (
                wide_ref[pl.ds(q + r, s.seq, s.block), :] * tw_cols[here, r : r + 1]
            ).astype(BF16)
    load.wait()
    inner_t = dot(unit(s.n2), inner_ref[...], 1, 1).astype(BF16)
    stores = []
    for r in range(s.rows):
        grad = dot(inner_t, col_ref[r], 1, 0)
        gained = grad * gain_ref[...]
        proj_ref[r : r + 1, :] = lane_sums(gained * x_ref[r].astype(F32))[0:1]
        sum_ref[r] = cot_ref[r].astype(F32) + inv_cols[:, r : r + 1] * gained
        stores.append(copies.start(sum_ref.at[r], sum_hbm.at[r]))
    wait(stores)


def finish_kernel(
    s, sum_hbm, whole_hbm, x_ref, inv_ref, proj_ref, out_hbm, weight_hbm, sum_ref, whole_ref, weight_ref, out_ref, sems
):
    copies = Copies(sems)
    whole_load = copies.start(whole_hbm, whole_ref)
    sum_loads = [copies.start(sum_hbm.at[r], sum_ref.at[r]) for r in range(s.rows)]
    inv = inv_ref[...]
    factor = column_form(inv * inv * inv * total(proj_ref) / D)
    whole_load.wait()
    for part in range(s.parts):
        weight_ref[:, part * LANES : (part + 1) * LANES] = whole_ref[pl.ds(part, s.width, s.parts), :]
    stores = [copies.start(weight_ref, weight_hbm)]
    for r in range(s.rows):
        sum_loads[r].wait()
        out_ref[r] = (sum_ref[r] - x_ref[r].astype(F32) * factor[:, r : r + 1]).astype(BF16)
        stores.append(copies.start(out_ref.at[r], out_hbm.at[r]))
    wait(stores)


HBM, AUTO = "hbm", "auto"


def call(kernel, s, name, outs, scratch, copies, flops, moved, *args):
    specs = {AUTO: pl.BlockSpec(memory_space=pltpu.VMEM), HBM: pl.BlockSpec(memory_space=pl.ANY)}
    return pl.pallas_call(
        functools.partial(kernel, s),
        out_shape=[
            (pltpu.HBM if place == HBM else jax.ShapeDtypeStruct)(shape, kind) for shape, kind, place in outs
        ],
        in_specs=[specs[place] for _, place in args],
        out_specs=[specs[place] for _, _, place in outs],
        scratch_shapes=[pltpu.VMEM(shape, kind) for shape, kind in scratch]
        + ([pltpu.SemaphoreType.DMA((copies,))] if copies else []),
        compiler_params=pltpu.CompilerParams(vmem_limit_bytes=24 << 20),
        cost_estimate=pl.CostEstimate(flops=flops, bytes_accessed=moved, transcendentals=0),
        name=name,
    )(*[pltpu.with_memory_space_constraint(v, pltpu.HBM) if place == HBM else v for v, place in args])


def exchange(v, seq):
    packed = v.reshape(seq, -1, LANES)
    return lax.all_to_all(packed, "seq", split_axis=0, concat_axis=0, tiled=True).reshape(v.shape)


def on_device(seq, inputs, norm_gain, inner_factor, outer_factor, twiddle, channel_weight, cotangent):
    rows, n2, width = inputs.shape
    s = Sizes(seq, rows, n2, width)
    packed_two = (2 * seq * s.block, LANES)
    groups = s.cols * s.parts + 1
    sent = (seq // 2, 2, groups, rows, LANES)
    mib = rows * n2 * width * 2
    flop = 2 * rows * n2 * n2 * width
    gain = norm_gain.reshape(1, width)
    small = (rows, n2)

    (part_sum,) = call(
        square_kernel, s, "squares", [(small, F32, AUTO)], [], 0, flop // 20, mib, (inputs, AUTO)
    )
    sums = lax.all_gather(part_sum, "chan")
    send, inv = call(
        inner_kernel, s, "inner", [(packed_two, BF16, AUTO), (small, F32, AUTO)],
        [(inputs.shape, BF16), (inner_factor.shape, BF16), (inputs.shape, BF16), (gain.shape, F32), (small, F32), (packed_two, F32)],
        4 + rows, flop, 5 * mib,
        (cotangent, HBM), (inner_factor, HBM), (inputs, HBM), (gain, HBM), (twiddle, HBM), (sums, AUTO),
    )
    got = exchange(send, seq)
    (back_send,) = call(
        middle_kernel, s, "middle", [(sent, BF16, AUTO)],
        [((s.parts * width, LANES), F32), ((rows * seq, LANES), F32)], 0, 3 * flop, 4 * mib,
        (got, AUTO), (channel_weight[0], AUTO), (outer_factor, AUTO),
    )
    back_got = lax.all_to_all(
        back_send.reshape(seq * groups, rows, LANES), "seq", split_axis=0, concat_axis=0, tiled=True
    ).reshape(sent)
    share = jnp.sum(back_got[:, :, -1].astype(F32), axis=(0, 1))
    whole = lax.all_to_all(
        jnp.broadcast_to(share, (seq,) + share.shape), "seq", split_axis=0, concat_axis=0, tiled=True
    )
    base, part_proj = call(
        back_kernel, s, "back", [(inputs.shape, F32, HBM), (small, F32, AUTO)],
        [(inner_factor.shape, BF16), (inputs.shape, F32), ((seq * s.block, LANES), F32), (inputs.shape, BF16)], 1 + rows, flop, 6 * mib,
        (inner_factor, HBM), (back_got, AUTO), (inputs, AUTO), (cotangent, AUTO), (inv, AUTO), (gain, AUTO), (twiddle, AUTO),
    )
    projections = lax.all_gather(part_proj, "chan")
    input_grad, weight_grad = call(
        finish_kernel, s, "finish", [(inputs.shape, BF16, HBM), ((width, width), F32, HBM)],
        [(inputs.shape, F32), ((s.parts * width, LANES), F32), ((width, width), F32), (inputs.shape, BF16)],
        2 * rows + 2, flop // 100, 4 * mib,
        (base, HBM), (whole.reshape(-1, LANES), HBM), (inputs, AUTO), (inv, AUTO), (projections, AUTO),
    )
    return (input_grad, weight_grad.reshape(1, width, width))


def solution(mesh):
    in_specs = (
        P("seq", None, "chan"),
        P("chan"),
        P(),
        P(),
        P("seq", None),
        P("chan", None, None),
        P("seq", None, "chan"),
    )
    out_specs = (P("seq", None, "chan"), P("chan", None, None))

    def run(*args):
        return on_device(mesh.shape["seq"], *args)

    return jax.shard_map(run, mesh=mesh, in_specs=in_specs, out_specs=out_specs, check_vma=False)
```

```python
import functools

import jax
import jax.numpy as jnp
from jax import lax
from jax.experimental import pallas as pl
from jax.experimental.pallas import tpu as pltpu
from jax.sharding import PartitionSpec as P

D = 1024
GELU_C = 0.7978845608028654
GELU_A = 0.044715
F32 = jnp.float32
BF16 = jnp.bfloat16
LANES = 128


def dot(a, b, ca, cb):
    return lax.dot_general(a, b, (((ca,), (cb,)), ((), ())), preferred_element_type=F32)


def lane_sums(v):
    ones = jnp.ones((8, v.shape[1]), BF16)
    hi = v.astype(BF16)
    rest = v - hi.astype(F32)
    return dot(ones, hi, 1, 1) + dot(ones, rest.astype(BF16), 1, 1)


def column_form(v):
    r, n = v.shape
    return jnp.concatenate([v] * (8 // r), axis=0).T


class Sizes:
    def __init__(self, seq, rows, n2, width):
        self.seq, self.rows, self.n2, self.width = seq, rows, n2, width
        self.cols = n2 // seq
        self.parts = width // LANES
        self.block = self.cols * self.parts * rows

    def pieces(self):
        for jh in range(self.cols):
            for part in range(self.parts):
                yield jh, part, (jh * self.parts + part) * self.rows


def total(ref):
    terms = [ref[k] for k in range(ref.shape[0])]
    while len(terms) > 1:
        terms = [a + b for a, b in zip(terms[::2], terms[1::2])]
    return terms[0]


class Copies:
    def __init__(self, sems):
        self.sems, self.count = sems, 0

    def start(self, source, target):
        copy = pltpu.make_async_copy(source, target, self.sems.at[self.count])
        copy.start()
        self.count += 1
        return copy

    def rows(self, source, target, count):
        return [self.start(source.at[r], target.at[r]) for r in range(count)]


def wait(copies):
    for copy in copies:
        copy.wait()


def square_kernel(s, x_ref, sum_ref):
    for r in range(s.rows):
        x = x_ref[r].astype(F32)
        sum_ref[r : r + 1, :] = lane_sums(x * x)[0:1]


def inner_kernel(
    s, cot_hbm, inner_hbm, x_hbm, gain_hbm, tw_hbm, sum_ref, send_ref, inv_ref,
    cot_ref, inner_ref, x_ref, gain_ref, tw_ref, wide_ref, sems,
):
    copies = Copies(sems)
    cot_loads = [copies.start(cot_hbm.at[r], cot_ref.at[r]) for r in range(s.rows)]
    tw_load = copies.start(tw_hbm, tw_ref)
    gain_load = copies.start(gain_hbm, gain_ref)
    inner_load = copies.start(inner_hbm, inner_ref)
    x_load = copies.start(x_hbm, x_ref)
    inv = lax.rsqrt(total(sum_ref) / D + 1e-05)
    inv_ref[...] = inv
    inv_cols = column_form(inv)
    for r in range(s.rows):
        cot_loads[r].wait()
        for jh, part, q in s.pieces():
            wide_ref[pl.ds(s.block + q + r, s.seq, 2 * s.block), :] = cot_ref[
                r, jh * s.seq : (jh + 1) * s.seq, part * LANES : (part + 1) * LANES
            ].astype(F32)
    wait([tw_load, gain_load, inner_load, x_load])
    tw_cols = column_form(tw_ref[...])
    for r in range(s.rows):
        normed = (x_ref[r].astype(F32) * inv_cols[:, r : r + 1] * gain_ref[...]).astype(BF16)
        y = dot(inner_ref[...], normed, 1, 0) * tw_cols[:, r : r + 1]
        for jh, part, q in s.pieces():
            wide_ref[pl.ds(q + r, s.seq, 2 * s.block), :] = y[
                jh * s.seq : (jh + 1) * s.seq, part * LANES : (part + 1) * LANES
            ]
    send_ref[...] = wide_ref[...].astype(BF16)


def swap_halves(first, second):
    low = lax.broadcasted_iota(jnp.int32, first.shape, 1) < 4
    return (
        jnp.where(low, first, pltpu.roll(second, 4, 1)),
        jnp.where(low, pltpu.roll(first, 4, 1), second),
    )


def put(out_ref, q, v):
    v = v.reshape(-1, 8, LANES)
    out_ref[:, 0, q] = v[:, :4].astype(BF16)
    out_ref[:, 1, q] = v[:, 4:].astype(BF16)


def middle_kernel(s, got_ref, weight_ref, outer_ref, send_ref, part_ref, piece_ref):
    n1 = s.seq * s.rows
    outer_t = outer_ref[...].T
    tiles = s.block // 8
    got = got_ref[...].reshape(s.seq // 2, 2, 2 * tiles, 8, LANES)
    for jh in range(s.cols):
        rot, cot = (
            jnp.concatenate(
                [
                    v.reshape(n1, LANES)
                    for v in swap_halves(got[:, 0, tile].astype(F32), got[:, 1, tile].astype(F32))
                ],
                axis=1,
            ).astype(BF16)
            for tile in (jh, tiles + jh)
        )
        v = dot(outer_ref[...], rot, 1, 0).astype(BF16).astype(F32)
        t = jnp.tanh(GELU_C * (v + GELU_A * v * v * v))
        hidden = (0.5 * v * (1.0 + t)).astype(BF16)
        slope = 0.5 * (1.0 + t) + 0.5 * v * (1.0 - t * t) * GELU_C * (1.0 + 3.0 * GELU_A * v * v)
        grad = (dot(cot, weight_ref[...], 1, 1) * slope).astype(BF16)
        product = dot(hidden, cot, 0, 0)
        for part in range(s.parts):
            here = slice(part * s.width, (part + 1) * s.width)
            term = product[:, part * LANES : (part + 1) * LANES]
            part_ref[here, :] = term if jh == 0 else part_ref[here, :] + term
        back = dot(outer_t, grad, 1, 0)
        for part in range(s.parts):
            put(send_ref, jh * s.parts + part, back[:, part * LANES : (part + 1) * LANES])
    step = s.width // s.seq
    for i in range(step):
        for part in range(s.parts):
            piece_ref[pl.ds(i * s.parts + part, s.seq, step * s.parts), :] = part_ref[
                pl.ds(part * s.width + i, s.seq, step), :
            ]
    put(send_ref, s.cols * s.parts, piece_ref[...])


def back_kernel(
    s, inner_hbm, got_ref, x_ref, cot_ref, inv_ref, gain_ref, tw_ref, sum_hbm, proj_ref,
    inner_ref, sum_ref, wide_ref, col_ref, sems,
):
    copies = Copies(sems)
    load = copies.start(inner_hbm, inner_ref)
    tiles = wide_ref.reshape(s.seq, s.block // 8, 8, LANES)
    for p in range(s.block // 8):
        both = [got_ref[:, :, q].astype(F32) for q in (2 * p, 2 * p + 1)]
        tiles[:, p] = jnp.concatenate(both, axis=2).reshape(s.seq, 8, LANES)
    inv_cols = column_form(inv_ref[...])
    tw_cols = column_form(tw_ref[...])
    for r in range(s.rows):
        for jh, part, q in s.pieces():
            here = slice(jh * s.seq, (jh + 1) * s.seq)
            col_ref[r, here, part * LANES : (part + 1) * LANES] = (
                wide_ref[pl.ds(q + r, s.seq, s.block), :] * tw_cols[here, r : r + 1]
            ).astype(BF16)
    load.wait()
    inner_t = inner_ref[...].T
    stores = []
    for r in range(s.rows):
        grad = dot(inner_t, col_ref[r], 1, 0)
        gained = grad * gain_ref[...]
        proj_ref[r : r + 1, :] = lane_sums(gained * x_ref[r].astype(F32))[0:1]
        sum_ref[r] = cot_ref[r].astype(F32) + inv_cols[:, r : r + 1] * gained
        stores.append(copies.start(sum_ref.at[r], sum_hbm.at[r]))
    wait(stores)


def finish_kernel(
    s, sum_hbm, whole_hbm, x_ref, inv_ref, proj_ref, out_hbm, weight_hbm, sum_ref, whole_ref, weight_ref, out_ref, sems
):
    copies = Copies(sems)
    whole_load = copies.start(whole_hbm, whole_ref)
    sum_loads = [copies.start(sum_hbm.at[r], sum_ref.at[r]) for r in range(s.rows)]
    inv = inv_ref[...]
    factor = column_form(inv * inv * inv * total(proj_ref) / D)
    whole_load.wait()
    for part in range(s.parts):
        weight_ref[:, part * LANES : (part + 1) * LANES] = whole_ref[pl.ds(part, s.width, s.parts), :]
    stores = [copies.start(weight_ref, weight_hbm)]
    for r in range(s.rows):
        sum_loads[r].wait()
        out_ref[r] = (sum_ref[r] - x_ref[r].astype(F32) * factor[:, r : r + 1]).astype(BF16)
        stores.append(copies.start(out_ref.at[r], out_hbm.at[r]))
    wait(stores)


HBM, AUTO = "hbm", "auto"


def call(kernel, s, name, outs, scratch, copies, flops, moved, *args):
    specs = {AUTO: pl.BlockSpec(memory_space=pltpu.VMEM), HBM: pl.BlockSpec(memory_space=pl.ANY)}
    return pl.pallas_call(
        functools.partial(kernel, s),
        out_shape=[
            (pltpu.HBM if place == HBM else jax.ShapeDtypeStruct)(shape, kind) for shape, kind, place in outs
        ],
        in_specs=[specs[place] for _, place in args],
        out_specs=[specs[place] for _, _, place in outs],
        scratch_shapes=[pltpu.VMEM(shape, kind) for shape, kind in scratch]
        + ([pltpu.SemaphoreType.DMA((copies,))] if copies else []),
        compiler_params=pltpu.CompilerParams(vmem_limit_bytes=24 << 20),
        cost_estimate=pl.CostEstimate(flops=flops, bytes_accessed=moved, transcendentals=0),
        name=name,
    )(*[pltpu.with_memory_space_constraint(v, pltpu.HBM) if place == HBM else v for v, place in args])


def exchange(v, seq):
    packed = v.reshape(seq, -1, LANES)
    return lax.all_to_all(packed, "seq", split_axis=0, concat_axis=0, tiled=True).reshape(v.shape)


def on_device(seq, inputs, norm_gain, inner_factor, outer_factor, twiddle, channel_weight, cotangent):
    rows, n2, width = inputs.shape
    s = Sizes(seq, rows, n2, width)
    packed_two = (2 * seq * s.block, LANES)
    groups = s.cols * s.parts + 1
    sent = (seq // 2, 2, groups, rows, LANES)
    mib = rows * n2 * width * 2
    flop = 2 * rows * n2 * n2 * width
    gain = norm_gain.reshape(1, width)
    small = (rows, n2)

    (part_sum,) = call(
        square_kernel, s, "squares", [(small, F32, AUTO)], [], 0, flop // 20, mib, (inputs, AUTO)
    )
    sums = lax.all_gather(part_sum, "chan")
    send, inv = call(
        inner_kernel, s, "inner", [(packed_two, BF16, AUTO), (small, F32, AUTO)],
        [(inputs.shape, BF16), (inner_factor.shape, BF16), (inputs.shape, BF16), (gain.shape, F32), (small, F32), (packed_two, F32)],
        4 + rows, flop, 5 * mib,
        (cotangent, HBM), (inner_factor, HBM), (inputs, HBM), (gain, HBM), (twiddle, HBM), (sums, AUTO),
    )
    got = exchange(send, seq)
    (back_send,) = call(
        middle_kernel, s, "middle", [(sent, BF16, AUTO)],
        [((s.parts * width, LANES), F32), ((rows * seq, LANES), F32)], 0, 3 * flop, 4 * mib,
        (got, AUTO), (channel_weight[0], AUTO), (outer_factor, AUTO),
    )
    back_got = lax.all_to_all(
        back_send.reshape(seq * groups, rows, LANES), "seq", split_axis=0, concat_axis=0, tiled=True
    ).reshape(sent)
    share = jnp.sum(back_got[:, :, -1].astype(F32), axis=(0, 1))
    whole = lax.all_to_all(
        jnp.broadcast_to(share, (seq,) + share.shape), "seq", split_axis=0, concat_axis=0, tiled=True
    )
    base, part_proj = call(
        back_kernel, s, "back", [(inputs.shape, F32, HBM), (small, F32, AUTO)],
        [(inner_factor.shape, BF16), (inputs.shape, F32), ((seq * s.block, LANES), F32), (inputs.shape, BF16)], 1 + rows, flop, 6 * mib,
        (inner_factor, HBM), (back_got, AUTO), (inputs, AUTO), (cotangent, AUTO), (inv, AUTO), (gain, AUTO), (twiddle, AUTO),
    )
    projections = lax.all_gather(part_proj, "chan")
    input_grad, weight_grad = call(
        finish_kernel, s, "finish", [(inputs.shape, BF16, HBM), ((width, width), F32, HBM)],
        [(inputs.shape, F32), ((s.parts * width, LANES), F32), ((width, width), F32), (inputs.shape, BF16)],
        2 * rows + 2, flop // 100, 4 * mib,
        (base, HBM), (whole.reshape(-1, LANES), HBM), (inputs, AUTO), (inv, AUTO), (projections, AUTO),
    )
    return (input_grad, weight_grad.reshape(1, width, width))


def solution(mesh):
    in_specs = (
        P("seq", None, "chan"),
        P("chan"),
        P(),
        P(),
        P("seq", None),
        P("chan", None, None),
        P("seq", None, "chan"),
    )
    out_specs = (P("seq", None, "chan"), P("chan", None, None))

    def run(*args):
        return on_device(mesh.shape["seq"], *args)

    return jax.shard_map(run, mesh=mesh, in_specs=in_specs, out_specs=out_specs, check_vma=False)
```
